32 devices in a mesh: groups: 2 (over x), gx: 8 (over z, y), gy: 2 (over core).
Axes of the slice: x: 2, y: 2, z: 4, core: 2. Of those that a mesh axis runs over, the one named last changes fastest.
Arguments:
- tokens: bfloat16 [512, 16384], P('groups', 'gx'), parts along dimension 0, may hold values from -6 to 6
- query_weight: bfloat16 [16384, 8, 2, 128], P('gx', None, 'gy'), may hold values from -0.046875 to 0.046875
- key_value_projection_weight: bfloat16 [16384, 2, 8, 128], P('gx'), may hold values from -0.046875 to 0.046875
- output_weight: bfloat16 [2048, 16384], P('gx', 'gy'), may hold values from -0.125 to 0.125
- document_ids: int32 [512], P('groups'), parts along dimension 0, may hold values from 0 to 7, never falling along the last dimension, each value on 1 to 64 neighbouring positions
- query_exponent: int32 [8, 2], P(None, 'gy'), may hold values from -11 to -8
- key_value_partial_exponents: int32 [2, 8], replicated, may hold values from -11 to -8
- key_value_summed_exponents: int32 [2, 8], replicated, may hold values from -7 to -5
- output_exponent: int32 [2, 64], P('gy'), may hold values from -13 to -10
- output_relevel: int32 [2, 64], P(None, 'gx'), may hold values from -10 to -8
Outputs:
- block_output: bfloat16 [512, 2, 8192], P('groups', None, 'gx'), parts along dimension 0
The draws below stay inside these ranges and needn't reach their ends.
There are 2 independent parts, one for each index of `groups`. The reference program is written for one: setup_inputs(seed, part) draws one part's arguments, and reference() takes and returns one part's arrays. A program takes and returns all parts, laid end to end along the dimension named above; an argument that names none is the same for every part. Nothing has to cross between parts.
Inputs may be any that keep to these rules, and one draw needn't show every extreme that they name: `document_ids`: never falling; each document is 1 to 64 tokens long, and one is exactly that long.
All inputs are finite; a program needn't handle non-finite values.
Results may differ from the reference program's by a relative error of at most 0.007.
Values may be sent and summed in bfloat16 or wider, within the bound.
A program may use at most 128 MiB of HBM per device.

```python
import math
import jax
import jax.numpy as jnp
import numpy as np
from jax import lax

MODEL_WIDTH = 16384
HEAD_SIZE = 128
KEY_VALUE_HEADS = 8
SPAN_TOKENS = 256
QUERY_HEADS = 16
NBH = 64
N_GX = 8


def set_ends(values, own_key, low, top_value):
    longest = values.shape.index(max(values.shape))
    spots = []
    for shift in (0, 1):
        where = [jax.random.randint(jax.random.fold_in(own_key, axis), (), 0, length) for axis, length in enumerate(values.shape)]
        where[longest] = (where[longest] + shift) % values.shape[longest]
        spots.append(tuple(where))
    return values.at[spots[0]].set(low).at[spots[1]].set(top_value)


def block_scale(own_key, shape, cuts, low, largest):
    gain = 1.0
    for dim, shards_of in cuts:
        heights = jax.random.uniform(jax.random.fold_in(jax.random.fold_in(own_key, 6), dim), (shards_of,), jnp.float32, low / len(cuts), largest / len(cuts))
        gain = gain * jnp.repeat(jnp.exp(heights), shape[dim] // shards_of).reshape((-1,) + (1,) * (len(shape) - 1 - dim))
    return gain


def length_profile(count, total, most, slope):
    loads = [(1 << 20) // math.isqrt(standing ** slope) + 1 for standing in range(2, count + 1)]
    surplus, given = total - most - (count - 1), [1] * (count - 1)
    while surplus > 0:
        movable = [i for i in range(count - 1) if given[i] < most]
        mass, left = sum([loads[i] for i in movable]), surplus
        for i in movable:
            extra = min(most - given[i], max(1, left * loads[i] // mass), surplus)
            given[i] = given[i] + extra
            surplus = surplus - extra
    return np.array([most] + given)


def ragged_sizes(rng, count, total, most, skew):
    if count == 2:
        one = jax.random.randint(rng, (), max(1, total - most), min(most, total - 1) + 1)
        return jnp.stack([one, total - one])
    sizes = jnp.asarray(length_profile(count, total, most, skew), jnp.int32)
    couples = (count - 1) // 2
    donor, receiver = sizes[1:1 + 2 * couples:2], sizes[2:2 + 2 * couples:2]
    room = jnp.minimum(donor - 1, most - receiver)
    passed = jax.random.randint(jax.random.fold_in(rng, 1), (couples,), 0, 1 << 20) % (room + 1)
    sizes = sizes.at[1:1 + 2 * couples:2].set(donor - passed).at[2:2 + 2 * couples:2].set(receiver + passed)
    return sizes[jax.random.permutation(jax.random.fold_in(rng, 2), count)]


def centred(key, dims, width, bound, shards=(), kind=jnp.bfloat16):
    result = width * jax.random.normal(key, dims, jnp.float32)
    if shards:
        result = result * block_scale(key, dims, shards, -0.22, 0.18)
    return jnp.clip(result, -bound, bound).astype(kind)


def setup_inputs(seed: int = 0, part: int = 0) -> dict:
    key_list = jax.random.split(jax.random.key(seed), 11)
    part_keys = jax.random.split(jax.random.fold_in(key_list[10], part), 11)
    return {
        "tokens": centred(part_keys[0], (SPAN_TOKENS, MODEL_WIDTH), 1.0, 6.0, ((1, 8),)),
        "query_weight": centred(key_list[1], (MODEL_WIDTH, QUERY_HEADS // 2, 2, HEAD_SIZE), MODEL_WIDTH ** -0.5, 0.046875, ((0, 8), (2, 2))),
        "key_value_projection_weight": centred(key_list[2], (MODEL_WIDTH, 2, KEY_VALUE_HEADS, HEAD_SIZE), MODEL_WIDTH ** -0.5, 0.046875, ((0, 8),)),
        "output_weight": centred(key_list[3], (QUERY_HEADS * HEAD_SIZE, MODEL_WIDTH), (QUERY_HEADS * HEAD_SIZE) ** -0.5, 0.125, ((0, 8), (1, 2))),
        "document_ids": jnp.searchsorted(jnp.cumsum(ragged_sizes(part_keys[4], 8, SPAN_TOKENS, SPAN_TOKENS // 4, 0)), jnp.arange(SPAN_TOKENS), side="right").astype(jnp.int32),
        "query_exponent": set_ends(jax.random.randint(key_list[5], (QUERY_HEADS // 2, 2), -11, -7), jax.random.fold_in(key_list[5], 1), -11, (-7) - 1).astype(jnp.int32),
        "key_value_partial_exponents": set_ends(jax.random.randint(key_list[6], (2, KEY_VALUE_HEADS), -11, -7), jax.random.fold_in(key_list[6], 1), -11, (-7) - 1).astype(jnp.int32),
        "key_value_summed_exponents": set_ends(jax.random.randint(key_list[7], (2, KEY_VALUE_HEADS), -7, -4), jax.random.fold_in(key_list[7], 1), -7, (-4) - 1).astype(jnp.int32),
        "output_exponent": set_ends(jax.random.randint(key_list[8], (2, NBH), -13, -9), jax.random.fold_in(key_list[8], 1), -13, (-9) - 1).astype(jnp.int32),
        "output_relevel": set_ends(jax.random.randint(key_list[9], (2, NBH), -10, -7), jax.random.fold_in(key_list[9], 1), -10, (-7) - 1).astype(jnp.int32),
    }


rotary_base = 500000.0
saturation = 127.0

def hadamard(order):
    row_index = jnp.arange(order, dtype=jnp.int32)[:, None]
    col_index = jnp.arange(order, dtype=jnp.int32)[None, :]
    common = row_index & col_index
    parity = jnp.zeros((order, order), jnp.int32)
    for bit_place in range(order.bit_length() - 1):
        parity = parity ^ common >> bit_place & 1
    return (1 - 2 * parity).astype(jnp.float32) * (1.0 / math.sqrt(order))

def rotate(values, rotation):
    return jnp.matmul(values, rotation, precision=lax.Precision.HIGHEST)

def rotary(values):
    length = values.shape[-2]
    full_width = values.shape[-1]
    half_width = full_width // 2
    frequency = rotary_base ** (-(jnp.arange(half_width, dtype=jnp.float32) * 2.0 / full_width))
    angles = jnp.arange(length, dtype=jnp.float32)[:, None] * frequency[None, :]
    cosine = jnp.cos(angles)
    sine_part = jnp.sin(angles)
    front_half = values[..., :half_width]
    back_half = values[..., half_width:]
    return jnp.concatenate([front_half * cosine - back_half * sine_part, back_half * cosine + front_half * sine_part], axis=-1)

def reference(tokens, query_weight, key_value_projection_weight, output_weight, document_ids, query_exponent, key_value_partial_exponents, key_value_summed_exponents, output_exponent, output_relevel):
    rotation = hadamard(HEAD_SIZE)
    piece_rows = MODEL_WIDTH // N_GX
    token_slices = tokens.reshape(SPAN_TOKENS, N_GX, piece_rows).transpose(1, 0, 2)
    query_slices = query_weight.reshape(N_GX, piece_rows, QUERY_HEADS // 2, 2, HEAD_SIZE)
    key_value_pieces = key_value_projection_weight.reshape(N_GX, piece_rows, 2, KEY_VALUE_HEADS, HEAD_SIZE)
    query_inverse = jnp.exp2(-query_exponent.astype(jnp.float32))
    keyvalue_inverse = jnp.exp2(-key_value_partial_exponents.astype(jnp.float32))

    def project(running, slices):
        token_slice, query_slice, keyvalue_slice = slices
        token_wide = token_slice.astype(jnp.float32)
        query_term = jnp.einsum('sd,dpme->pmse', token_wide, query_slice.astype(jnp.float32), precision=lax.Precision.HIGHEST)
        query_term = jnp.clip(rotate(query_term, rotation) * query_inverse[:, :, None, None], -saturation, saturation)
        memory_term = jnp.einsum('sd,dche->chse', token_wide, keyvalue_slice.astype(jnp.float32), precision=lax.Precision.HIGHEST)
        memory_term = jnp.clip(rotate(memory_term, rotation) * keyvalue_inverse[:, :, None, None], -saturation, saturation)
        return ((running[0] + query_term, running[1] + memory_term), None)
    initial_carry = (jnp.zeros((QUERY_HEADS // 2, 2, SPAN_TOKENS, HEAD_SIZE), jnp.float32), jnp.zeros((2, KEY_VALUE_HEADS, SPAN_TOKENS, HEAD_SIZE), jnp.float32))
    (query_sum, keyvalue_sum), _ = lax.scan(project, initial_carry, (token_slices, query_slices, key_value_pieces))
    query = rotate(query_sum * jnp.exp2(query_exponent.astype(jnp.float32))[:, :, None, None], rotation)
    query = rotary(query).astype(jnp.bfloat16).reshape(QUERY_HEADS, SPAN_TOKENS, HEAD_SIZE)
    memory_scale = jnp.exp2(key_value_summed_exponents.astype(jnp.float32))[:, :, None, None]
    keyvalue_level = jnp.clip(keyvalue_sum * jnp.exp2(key_value_partial_exponents.astype(jnp.float32))[:, :, None, None] / memory_scale, -saturation, saturation)
    keyvalue_full = rotate(keyvalue_level * memory_scale, rotation)
    keys = rotary(keyvalue_full[0]).astype(jnp.bfloat16)
    values = keyvalue_full[1].astype(jnp.bfloat16)
    shared_group = QUERY_HEADS // KEY_VALUE_HEADS
    keys = jnp.repeat(keys, shared_group, axis=0)
    values = jnp.repeat(values, shared_group, axis=0)
    scores = jnp.einsum('hqe,hke->hqk', query.astype(jnp.float32), keys.astype(jnp.float32), precision=lax.Precision.HIGHEST) * (1.0 / math.sqrt(HEAD_SIZE))
    position = jnp.arange(SPAN_TOKENS, dtype=jnp.int32)
    allowed = (position[:, None] >= position[None, :]) & (document_ids[:, None] == document_ids[None, :])
    scores = jnp.where(allowed[None], scores, -jnp.inf)
    row_max = lax.optimization_barrier(jnp.max(scores, axis=-1, keepdims=True))
    exponentials = jnp.exp(scores - row_max)
    weights = (exponentials / lax.optimization_barrier(jnp.sum(exponentials, axis=-1, keepdims=True))).astype(jnp.bfloat16)
    attended = jnp.einsum('hqk,hke->hqe', weights.astype(jnp.float32), values.astype(jnp.float32), precision=lax.Precision.HIGHEST).astype(jnp.bfloat16)
    mixed = attended.transpose(1, 0, 2).reshape(SPAN_TOKENS, N_GX, 2 * HEAD_SIZE).transpose(1, 0, 2)
    output_slices = output_weight.reshape(N_GX, 2 * HEAD_SIZE, MODEL_WIDTH)
    output_inverse = jnp.exp2(-output_exponent.astype(jnp.float32))

    def gather_output(running, slices):
        mixed_slice, weight_slice = slices
        out_term = jnp.dot(mixed_slice.astype(jnp.float32), weight_slice.astype(jnp.float32), precision=lax.Precision.HIGHEST).reshape(SPAN_TOKENS, 2, NBH, HEAD_SIZE)
        out_term = jnp.clip(rotate(out_term, rotation) * output_inverse[None, :, :, None], -saturation, saturation)
        return (running + out_term, None)
    out_sum, _ = lax.scan(gather_output, jnp.zeros((SPAN_TOKENS, 2, NBH, HEAD_SIZE), jnp.float32), (mixed, output_slices))
    out_scale = jnp.exp2(output_relevel.astype(jnp.float32))[None, :, :, None]
    out_level = jnp.clip(out_sum * jnp.exp2(output_exponent.astype(jnp.float32))[None, :, :, None] / out_scale, -saturation, saturation)
    return rotate(out_level * out_scale, rotation).reshape(SPAN_TOKENS, 2, MODEL_WIDTH // 2).astype(jnp.bfloat16)
```

```python
import functools
import math

import jax
import jax.numpy as jnp
import numpy as np
from jax import lax
from jax.experimental import pallas as pl
from jax.experimental.pallas import tpu as pltpu
from jax.sharding import PartitionSpec as P

rotary_base = 500000.0
saturation = 127.0


def hadamard(order):
    row_index = jnp.arange(order, dtype=jnp.int32)[:, None]
    col_index = jnp.arange(order, dtype=jnp.int32)[None, :]
    common = row_index & col_index
    parity = jnp.zeros((order, order), jnp.int32)
    for bit_place in range(order.bit_length() - 1):
        parity = parity ^ common >> bit_place & 1
    return (1 - 2 * parity).astype(jnp.float32) * (1.0 / math.sqrt(order))


def rotate(values, rotation):
    return jnp.matmul(values, rotation, precision=lax.Precision.HIGHEST)


def rotary(values):
    length = values.shape[-2]
    full_width = values.shape[-1]
    half_width = full_width // 2
    frequency = rotary_base ** (-(jnp.arange(half_width, dtype=jnp.float32) * 2.0 / full_width))
    places = jnp.arange(length, dtype=jnp.int32).astype(jnp.float32)
    angles = places[:, None] * frequency[None, :]
    cosine = jnp.cos(angles)
    sine_part = jnp.sin(angles)
    front_half = values[..., :half_width]
    back_half = values[..., half_width:]
    return jnp.concatenate(
        [front_half * cosine - back_half * sine_part, back_half * cosine + front_half * sine_part],
        axis=-1,
    )


def plain_body(
    tokens,
    query_weight,
    key_value_projection_weight,
    output_weight,
    document_ids,
    query_exponent,
    key_value_partial_exponents,
    key_value_summed_exponents,
    output_exponent,
    output_relevel,
):
    length = tokens.shape[0]
    head_width = query_weight.shape[3]
    memory_heads = key_value_projection_weight.shape[2]
    count_gx = lax.axis_size("gx")
    where_gx = lax.axis_index("gx")
    where_gy = lax.axis_index("gy")
    rotation = hadamard(head_width)
    query_block = query_weight[:, :, 0, :]
    query_inverse = jnp.exp2(-query_exponent[:, 0].astype(jnp.float32))
    query_up = jnp.exp2(query_exponent[:, 0].astype(jnp.float32))
    heads_total = query_block.shape[1]
    heads_here = heads_total // count_gx
    heads_spread = count_gx // memory_heads
    memory_index = where_gx // heads_spread
    memory_inverse = jnp.exp2(-key_value_partial_exponents.astype(jnp.float32))
    memory_up = jnp.exp2(key_value_partial_exponents.astype(jnp.float32))
    memory_scale = jnp.exp2(key_value_summed_exponents.astype(jnp.float32))
    partial_sum = jnp.einsum("sd,dpe->pse", tokens, query_block, preferred_element_type=jnp.float32)
    factor = query_inverse
    query_sum = lax.psum_scatter(
        jnp.clip(rotate(partial_sum, rotation) * factor[:, None, None], -saturation, saturation),
        "gx",
        scatter_dimension=0,
        tiled=True,
    )
    query_scale = lax.dynamic_slice_in_dim(query_up, where_gx * heads_here, heads_here, 0)
    query = rotary(rotate(query_sum * query_scale[:, None, None], rotation))[0].astype(jnp.bfloat16)
    partial_sum = jnp.einsum(
        "sd,dche->sche", tokens, key_value_projection_weight, preferred_element_type=jnp.float32
    )
    memory_sum = lax.psum_scatter(
        jnp.clip(
            rotate(partial_sum, rotation) * memory_inverse[None, :, :, None],
            -saturation,
            saturation,
        ),
        "gx",
        scatter_dimension=0,
        tiled=True,
    )
    whole = lax.all_gather(
        jnp.clip(
            memory_sum * memory_up[None, :, :, None] / memory_scale[None, :, :, None],
            -saturation,
            saturation,
        ),
        "gx",
        axis=0,
        tiled=True,
    )
    arrived = lax.dynamic_index_in_dim(whole, memory_index, 2, keepdims=False)
    head_scale = lax.dynamic_index_in_dim(memory_scale, memory_index, 1, keepdims=False)
    memory_full = rotate(arrived * head_scale[None, :, None], rotation)
    keys = rotary(memory_full[:, 0]).astype(jnp.bfloat16)
    values = memory_full[:, 1].astype(jnp.bfloat16)
    scores = jnp.einsum("qe,ke->qk", query, keys, preferred_element_type=jnp.float32) * (
        1.0 / math.sqrt(head_width)
    )
    position = jnp.arange(length, dtype=jnp.int32)
    allowed = (position[:, None] >= position[None, :]) & (
        document_ids[:, None] == document_ids[None, :]
    )
    scores = jnp.where(allowed, scores, -jnp.inf)
    row_max = jnp.max(scores, axis=-1, keepdims=True)
    exponentials = jnp.exp(scores - row_max)
    weights = (exponentials / jnp.sum(exponentials, axis=-1, keepdims=True)).astype(jnp.bfloat16)
    attended = jnp.dot(weights, values, preferred_element_type=jnp.float32).astype(jnp.bfloat16)
    head_pairs = lax.all_gather(attended, "gy", axis=1, tiled=True)
    feature_blocks = output_weight.shape[1] // head_width
    blocks_here = feature_blocks // count_gx
    output_inverse = jnp.exp2(-output_exponent[0].astype(jnp.float32))
    partial_sum = jnp.dot(head_pairs, output_weight, preferred_element_type=jnp.float32)
    partial_sum = partial_sum.reshape(
        length, blocks_here * lax.axis_size("gx"), head_width
    ).transpose(1, 0, 2)
    factor = output_inverse
    out_sum = lax.psum_scatter(
        jnp.clip(rotate(partial_sum, rotation) * factor[:, None, None], -saturation, saturation),
        "gx",
        scatter_dimension=0,
        tiled=True,
    )
    out_up = jnp.exp2(
        lax.dynamic_slice_in_dim(output_exponent[0], where_gx * blocks_here, blocks_here, 0).astype(
            jnp.float32
        )
    )
    own_scale = jnp.exp2(
        lax.dynamic_index_in_dim(output_relevel, where_gy, 0, keepdims=False).astype(jnp.float32)
    )
    out_level = jnp.clip(
        out_sum * out_up[:, None, None] / own_scale[:, None, None], -saturation, saturation
    )
    halves = lax.all_gather(out_level[None], "gy", axis=0, tiled=True)
    restored = rotate(
        halves * jnp.exp2(output_relevel.astype(jnp.float32))[:, :, None, None], rotation
    )
    return (
        restored.transpose(2, 0, 1, 3)
        .reshape(length, 2, blocks_here * head_width)
        .astype(jnp.bfloat16)
    )


def signs(order):
    index = np.arange(order)
    common = index[:, None] & index[None, :]
    parity = np.zeros((order, order), np.int64)
    for place in range(order.bit_length() - 1):
        parity ^= (common >> place) & 1
    return 1.0 - 2.0 * parity


def paired_signs(order):
    return np.kron(np.eye(2), signs(order))


def rotary_tables(length, width):
    half = width // 2
    frequency = rotary_base ** (-(np.arange(half, dtype=np.float64) * 2.0 / width))
    angles = np.arange(length)[:, None] * frequency.astype(np.float32).astype(np.float64)[None, :]
    cosine = np.concatenate([np.cos(angles), np.cos(angles)], axis=1)
    sine = np.concatenate([-np.sin(angles), np.sin(angles)], axis=1)
    return (
        np.stack([cosine, np.ones_like(cosine)]).astype(np.float32),
        np.stack([sine, np.zeros_like(sine)]).astype(np.float32),
    )


def turn(values, sign_matrix, norm):
    upper = values.astype(jnp.bfloat16)
    lower = (values - upper.astype(jnp.float32)).astype(jnp.bfloat16)
    total = jnp.dot(upper, sign_matrix, preferred_element_type=jnp.float32)
    total = total + jnp.dot(lower, sign_matrix, preferred_element_type=jnp.float32)
    return total * norm


def saturate(values):
    return jnp.clip(values, -saturation, saturation)


def fused_kernel(
    count,
    query_part,
    memory_part,
    out_weight_hbm,
    first_scale,
    own_scale,
    out_inverse,
    out_ratio,
    out_scale,
    sign_ref,
    cosine_ref,
    sine_ref,
    document_column,
    document_row,
    out_ref,
    out_weight,
    first_send,
    first_recv,
    memory_pair,
    mixed,
    second_send,
    second_recv,
    total,
    weight_sem,
    first_send_sem,
    first_recv_sem,
    second_send_sem,
    second_recv_sem,
    pair_send_sem,
    pair_recv_sem,
):
    me = lax.axis_index("gx")
    core = lax.axis_index("gy")
    mate = 1 - core
    length, width = query_part.shape[1], query_part.shape[2]
    span = out_inverse.shape[2]
    norm = 1.0 / math.sqrt(width)
    chunk = 2 * width

    load = pltpu.make_async_copy(out_weight_hbm, out_weight, weight_sem)
    load.start()

    barrier = pltpu.get_barrier_semaphore()
    for away in range(1, count):
        pl.semaphore_signal(
            barrier,
            inc=1,
            device_id={"gx": lax.rem(me + away, count)},
            device_id_type=pl.DeviceIdType.MESH,
        )
    pl.semaphore_signal(
        barrier, inc=1, device_id={"gy": mate}, device_id_type=pl.DeviceIdType.MESH
    )
    pl.semaphore_wait(barrier, count)

    small_signs = sign_ref[:width, :width]

    def first_copy(away):
        return pltpu.make_async_remote_copy(
            src_ref=first_send.at[away],
            dst_ref=first_recv.at[away],
            send_sem=first_send_sem.at[away],
            recv_sem=first_recv_sem.at[away],
            device_id={"gx": lax.rem(me + away, count)},
            device_id_type=pl.DeviceIdType.MESH,
        )

    def second_copy(away):
        return pltpu.make_async_remote_copy(
            src_ref=second_send.at[away],
            dst_ref=second_recv.at[away],
            send_sem=second_send_sem.at[away],
            recv_sem=second_recv_sem.at[away],
            device_id={"gx": lax.rem(me + away, count)},
            device_id_type=pl.DeviceIdType.MESH,
        )

    def pair_copy(ref, place):
        return pltpu.make_async_remote_copy(
            src_ref=ref.at[core],
            dst_ref=ref.at[core],
            send_sem=pair_send_sem.at[place],
            recv_sem=pair_recv_sem.at[place],
            device_id={"gy": mate},
            device_id_type=pl.DeviceIdType.MESH,
        )

    def first_term(target):
        query = saturate(turn(query_part[target], small_signs, norm) * first_scale[target, 0:1, :])
        memory = saturate(
            turn(memory_part[target], small_signs, norm) * first_scale[target, 1:2, :]
        )
        return query, memory

    def first_step(away, carry):
        query, memory = first_term(lax.rem(me + away, count))
        first_send[away, 0] = query.astype(jnp.bfloat16)
        first_send[away, 1] = memory.astype(jnp.bfloat16)
        first_copy(away).start()
        return carry

    lax.fori_loop(1, count, first_step, 0)
    query, memory = first_term(me)
    total[:, :width] = query
    total[:, width : 2 * width] = memory

    def first_sum(away, carry):
        first_copy(away).wait_recv()
        total[:, :width] += first_recv[away, 0].astype(jnp.float32)
        total[:, width : 2 * width] += first_recv[away, 1].astype(jnp.float32)
        return carry

    lax.fori_loop(1, count, first_sum, 0)

    level = saturate(total[:, width : 2 * width] * own_scale[1:2, :])
    memory = turn(level * own_scale[2:3, :], small_signs, norm)
    memory = memory * cosine_ref[core] + pltpu.roll(memory, width // 2, 1) * sine_ref[core]
    memory_pair[core] = memory.astype(jnp.bfloat16)
    pair_copy(memory_pair, 0).start()
    query = turn(total[:, :width] * own_scale[0:1, :], small_signs, norm)
    query = query * cosine_ref[0] + pltpu.roll(query, width // 2, 1) * sine_ref[0]
    query = query.astype(jnp.bfloat16)
    pair_copy(memory_pair, 0).wait_recv()

    scores = lax.dot_general(
        query, memory_pair[0], (((1,), (1,)), ((), ())), preferred_element_type=jnp.float32
    ) * (1.0 / math.sqrt(width))
    rows = lax.broadcasted_iota(jnp.int32, (length, length), 0)
    columns = lax.broadcasted_iota(jnp.int32, (length, length), 1)
    allowed = (rows >= columns) & (document_column[...] == document_row[...])
    scores = jnp.where(allowed, scores, -jnp.inf)
    exponentials = jnp.exp(scores - jnp.max(scores, axis=-1, keepdims=True))
    weights = exponentials / jnp.sum(exponentials, axis=-1, keepdims=True)
    mixed[core] = jnp.dot(
        weights.astype(jnp.bfloat16), memory_pair[1], preferred_element_type=jnp.float32
    ).astype(jnp.bfloat16)
    pair_copy(mixed, 1).start()
    load.wait()
    pair_copy(mixed, 1).wait_recv()

    def second_term(target, part):
        start = pl.multiple_of(target * span + part * chunk, chunk)
        both = jnp.concatenate([mixed[0], mixed[1]], axis=1)
        product = jnp.dot(
            both, out_weight[:, pl.ds(start, chunk)], preferred_element_type=jnp.float32
        )
        scale = out_inverse[target, :, part * chunk : (part + 1) * chunk]
        return saturate(turn(product, sign_ref[...], norm) * scale)

    def second_step(away, carry):
        target = lax.rem(me + away, count)
        for part in range(span // chunk):
            second_send[away, :, part * chunk : (part + 1) * chunk] = second_term(
                target, part
            ).astype(jnp.bfloat16)
        second_copy(away).start()
        return carry

    lax.fori_loop(1, count, second_step, 0)
    for part in range(span // chunk):
        total[:, part * chunk : (part + 1) * chunk] = second_term(me, part)

    def second_sum(away, carry):
        second_copy(away).wait_recv()
        for part in range(span // chunk):
            place = slice(part * chunk, (part + 1) * chunk)
            total[:, place] += second_recv[away, :, place].astype(jnp.float32)
        return carry

    lax.fori_loop(1, count, second_sum, 0)
    for part in range(span // chunk):
        place = slice(part * chunk, (part + 1) * chunk)
        level = saturate(total[:, place] * out_ratio[:, place])
        out_ref[core, :, place] = turn(level * out_scale[:, place], sign_ref[...], norm).astype(
            jnp.bfloat16
        )
    pair_copy(out_ref, 2).start()

    def drain(away, carry):
        first_copy(away).wait_send()
        second_copy(away).wait_send()
        return carry

    lax.fori_loop(1, count, drain, 0)
    pair_copy(memory_pair, 0).wait_send()
    pair_copy(mixed, 1).wait_send()
    pair_copy(out_ref, 2).wait()


def body(
    tokens,
    query_weight,
    key_value_projection_weight,
    output_weight,
    document_ids,
    query_exponent,
    key_value_partial_exponents,
    key_value_summed_exponents,
    output_exponent,
    output_relevel,
):
    count = lax.axis_size("gx")
    length = tokens.shape[0]
    width = query_weight.shape[3]
    heads = query_weight.shape[1]
    memory_heads = key_value_projection_weight.shape[2]
    span = output_weight.shape[1] // count
    if not (count == heads == memory_heads and lax.axis_size("gy") == 2 and span % (2 * width) == 0):
        return plain_body(
            tokens,
            query_weight,
            key_value_projection_weight,
            output_weight,
            document_ids,
            query_exponent,
            key_value_partial_exponents,
            key_value_summed_exponents,
            output_exponent,
            output_relevel,
        )
    me = lax.axis_index("gx")
    core = lax.axis_index("gy")
    memory_weight = lax.dynamic_index_in_dim(key_value_projection_weight, core, 1, keepdims=False)
    query_part = jnp.einsum(
        "sd,dpe->pse", tokens, query_weight[:, :, 0, :], preferred_element_type=jnp.float32
    )
    memory_part = jnp.einsum("sd,dne->nse", tokens, memory_weight, preferred_element_type=jnp.float32)

    def power(exponent):
        return jnp.exp2(exponent.astype(jnp.float32))

    partial_exponent = lax.dynamic_index_in_dim(key_value_partial_exponents, core, 0, keepdims=False)
    summed_exponent = lax.dynamic_index_in_dim(key_value_summed_exponents, core, 0, keepdims=False)
    first_scale = jnp.broadcast_to(
        power(-jnp.stack([query_exponent[:, 0], partial_exponent], axis=1))[:, :, None],
        (count, 2, width),
    )
    own = jnp.stack(
        [query_exponent[:, 0], partial_exponent - summed_exponent, summed_exponent], axis=0
    )
    own = lax.dynamic_index_in_dim(own, me, 1, keepdims=True)
    own_scale = jnp.broadcast_to(power(own), (3, width))
    blocks = span // width
    out_inverse = jnp.repeat(power(-output_exponent[0]), width).reshape(count, 1, span)
    relevel = lax.dynamic_index_in_dim(output_relevel, core, 0, keepdims=False)
    here = lax.dynamic_slice_in_dim(output_exponent[0], me * blocks, blocks, 0)
    out_ratio = jnp.repeat(power(here - relevel), width)[None]
    out_scale = jnp.repeat(power(relevel), width)[None]
    cosine, sine = rotary_tables(length, width)
    vmem = pl.BlockSpec(memory_space=pltpu.VMEM)
    halves = pl.pallas_call(
        functools.partial(fused_kernel, count),
        out_shape=jax.ShapeDtypeStruct((2, length, span), jnp.bfloat16),
        in_specs=[vmem, vmem, pl.BlockSpec(memory_space=pl.ANY)] + [vmem] * 10,
        out_specs=vmem,
        scratch_shapes=[
            pltpu.VMEM(output_weight.shape, jnp.bfloat16),
            pltpu.VMEM((count, 2, length, width), jnp.bfloat16),
            pltpu.VMEM((count, 2, length, width), jnp.bfloat16),
            pltpu.VMEM((2, length, width), jnp.bfloat16),
            pltpu.VMEM((2, length, width), jnp.bfloat16),
            pltpu.VMEM((count, length, span), jnp.bfloat16),
            pltpu.VMEM((count, length, span), jnp.bfloat16),
            pltpu.VMEM((length, span), jnp.float32),
            pltpu.SemaphoreType.DMA,
            pltpu.SemaphoreType.DMA((count,)),
            pltpu.SemaphoreType.DMA((count,)),
            pltpu.SemaphoreType.DMA((count,)),
            pltpu.SemaphoreType.DMA((count,)),
            pltpu.SemaphoreType.DMA((3,)),
            pltpu.SemaphoreType.DMA((3,)),
        ],
        compiler_params=pltpu.CompilerParams(
            collective_id=0, has_side_effects=True, vmem_limit_bytes=40 * 1024 * 1024
        ),
    )(
        query_part,
        memory_part,
        output_weight,
        first_scale,
        own_scale,
        out_inverse,
        out_ratio,
        out_scale,
        jnp.asarray(paired_signs(width), jnp.bfloat16),
        jnp.asarray(cosine),
        jnp.asarray(sine),
        document_ids[:, None],
        document_ids[None, :],
    )
    return halves.transpose(1, 0, 2)


def solution(mesh):
    return jax.shard_map(
        body,
        mesh=mesh,
        in_specs=(
            P("groups", "gx"),
            P("gx", None, "gy", None),
            P("gx", None, None, None),
            P("gx", "gy"),
            P("groups"),
            P(None, "gy"),
            P(),
            P(),
            P("gy", None),
            P(None, "gx"),
        ),
        out_specs=P("groups", None, "gx"),
        check_vma=False,
    )
```

```python
import functools
import math

import jax
import jax.numpy as jnp
import numpy as np
from jax import lax
from jax.experimental import pallas as pl
from jax.experimental.pallas import tpu as pltpu
from jax.sharding import PartitionSpec as P

rotary_base = 500000.0
saturation = 127.0


def hadamard(order):
    row_index = jnp.arange(order, dtype=jnp.int32)[:, None]
    col_index = jnp.arange(order, dtype=jnp.int32)[None, :]
    common = row_index & col_index
    parity = jnp.zeros((order, order), jnp.int32)
    for bit_place in range(order.bit_length() - 1):
        parity = parity ^ common >> bit_place & 1
    return (1 - 2 * parity).astype(jnp.float32) * (1.0 / math.sqrt(order))


def rotate(values, rotation):
    return jnp.matmul(values, rotation, precision=lax.Precision.HIGHEST)


def rotary(values):
    length = values.shape[-2]
    full_width = values.shape[-1]
    half_width = full_width // 2
    frequency = rotary_base ** (-(jnp.arange(half_width, dtype=jnp.float32) * 2.0 / full_width))
    places = jnp.arange(length, dtype=jnp.int32).astype(jnp.float32)
    angles = places[:, None] * frequency[None, :]
    cosine = jnp.cos(angles)
    sine_part = jnp.sin(angles)
    front_half = values[..., :half_width]
    back_half = values[..., half_width:]
    return jnp.concatenate(
        [front_half * cosine - back_half * sine_part, back_half * cosine + front_half * sine_part],
        axis=-1,
    )


def plain_body(
    tokens,
    query_weight,
    key_value_projection_weight,
    output_weight,
    document_ids,
    query_exponent,
    key_value_partial_exponents,
    key_value_summed_exponents,
    output_exponent,
    output_relevel,
):
    length = tokens.shape[0]
    head_width = query_weight.shape[3]
    memory_heads = key_value_projection_weight.shape[2]
    count_gx = lax.axis_size("gx")
    where_gx = lax.axis_index("gx")
    where_gy = lax.axis_index("gy")
    rotation = hadamard(head_width)
    query_block = query_weight[:, :, 0, :]
    query_inverse = jnp.exp2(-query_exponent[:, 0].astype(jnp.float32))
    query_up = jnp.exp2(query_exponent[:, 0].astype(jnp.float32))
    heads_total = query_block.shape[1]
    heads_here = heads_total // count_gx
    heads_spread = count_gx // memory_heads
    memory_index = where_gx // heads_spread
    memory_inverse = jnp.exp2(-key_value_partial_exponents.astype(jnp.float32))
    memory_up = jnp.exp2(key_value_partial_exponents.astype(jnp.float32))
    memory_scale = jnp.exp2(key_value_summed_exponents.astype(jnp.float32))
    partial_sum = jnp.einsum("sd,dpe->pse", tokens, query_block, preferred_element_type=jnp.float32)
    factor = query_inverse
    query_sum = lax.psum_scatter(
        jnp.clip(rotate(partial_sum, rotation) * factor[:, None, None], -saturation, saturation),
        "gx",
        scatter_dimension=0,
        tiled=True,
    )
    query_scale = lax.dynamic_slice_in_dim(query_up, where_gx * heads_here, heads_here, 0)
    query = rotary(rotate(query_sum * query_scale[:, None, None], rotation))[0].astype(jnp.bfloat16)
    partial_sum = jnp.einsum(
        "sd,dche->sche", tokens, key_value_projection_weight, preferred_element_type=jnp.float32
    )
    memory_sum = lax.psum_scatter(
        jnp.clip(
            rotate(partial_sum, rotation) * memory_inverse[None, :, :, None],
            -saturation,
            saturation,
        ),
        "gx",
        scatter_dimension=0,
        tiled=True,
    )
    whole = lax.all_gather(
        jnp.clip(
            memory_sum * memory_up[None, :, :, None] / memory_scale[None, :, :, None],
            -saturation,
            saturation,
        ),
        "gx",
        axis=0,
        tiled=True,
    )
    arrived = lax.dynamic_index_in_dim(whole, memory_index, 2, keepdims=False)
    head_scale = lax.dynamic_index_in_dim(memory_scale, memory_index, 1, keepdims=False)
    memory_full = rotate(arrived * head_scale[None, :, None], rotation)
    keys = rotary(memory_full[:, 0]).astype(jnp.bfloat16)
    values = memory_full[:, 1].astype(jnp.bfloat16)
    scores = jnp.einsum("qe,ke->qk", query, keys, preferred_element_type=jnp.float32) * (
        1.0 / math.sqrt(head_width)
    )
    position = jnp.arange(length, dtype=jnp.int32)
    allowed = (position[:, None] >= position[None, :]) & (
        document_ids[:, None] == document_ids[None, :]
    )
    scores = jnp.where(allowed, scores, -jnp.inf)
    row_max = jnp.max(scores, axis=-1, keepdims=True)
    exponentials = jnp.exp(scores - row_max)
    weights = (exponentials / jnp.sum(exponentials, axis=-1, keepdims=True)).astype(jnp.bfloat16)
    attended = jnp.dot(weights, values, preferred_element_type=jnp.float32).astype(jnp.bfloat16)
    head_pairs = lax.all_gather(attended, "gy", axis=1, tiled=True)
    feature_blocks = output_weight.shape[1] // head_width
    blocks_here = feature_blocks // count_gx
    output_inverse = jnp.exp2(-output_exponent[0].astype(jnp.float32))
    partial_sum = jnp.dot(head_pairs, output_weight, preferred_element_type=jnp.float32)
    partial_sum = partial_sum.reshape(
        length, blocks_here * lax.axis_size("gx"), head_width
    ).transpose(1, 0, 2)
    factor = output_inverse
    out_sum = lax.psum_scatter(
        jnp.clip(rotate(partial_sum, rotation) * factor[:, None, None], -saturation, saturation),
        "gx",
        scatter_dimension=0,
        tiled=True,
    )
    out_up = jnp.exp2(
        lax.dynamic_slice_in_dim(output_exponent[0], where_gx * blocks_here, blocks_here, 0).astype(
            jnp.float32
        )
    )
    own_scale = jnp.exp2(
        lax.dynamic_index_in_dim(output_relevel, where_gy, 0, keepdims=False).astype(jnp.float32)
    )
    out_level = jnp.clip(
        out_sum * out_up[:, None, None] / own_scale[:, None, None], -saturation, saturation
    )
    halves = lax.all_gather(out_level[None], "gy", axis=0, tiled=True)
    restored = rotate(
        halves * jnp.exp2(output_relevel.astype(jnp.float32))[:, :, None, None], rotation
    )
    return (
        restored.transpose(2, 0, 1, 3)
        .reshape(length, 2, blocks_here * head_width)
        .astype(jnp.bfloat16)
    )


def signs(order):
    index = np.arange(order)
    common = index[:, None] & index[None, :]
    parity = np.zeros((order, order), np.int64)
    for place in range(order.bit_length() - 1):
        parity ^= (common >> place) & 1
    return 1.0 - 2.0 * parity


def paired_signs(order):
    return np.kron(np.eye(2), signs(order))


def rotary_tables(length, width):
    half = width // 2
    frequency = rotary_base ** (-(np.arange(half, dtype=np.float64) * 2.0 / width))
    angles = np.arange(length)[:, None] * frequency.astype(np.float32).astype(np.float64)[None, :]
    cosine = np.concatenate([np.cos(angles), np.cos(angles)], axis=1)
    sine = np.concatenate([-np.sin(angles), np.sin(angles)], axis=1)
    return cosine.astype(np.float32), sine.astype(np.float32)


def power(exponent, width):
    row = jnp.full((1, width), exponent, jnp.int32)
    size = jnp.abs(row)
    upward = jnp.ones((1, width), jnp.float32)
    downward = jnp.ones((1, width), jnp.float32)
    for place in (1, 2, 4, 8, 16):
        taken = (size & place) != 0
        upward = jnp.where(taken, upward * 2.0**place, upward)
        downward = jnp.where(taken, downward * 2.0**-place, downward)
    return jnp.where(row >= 0, upward, downward)


def turn(values, sign_matrix, norm):
    upper = values.astype(jnp.bfloat16)
    lower = (values - upper.astype(jnp.float32)).astype(jnp.bfloat16)
    total = jnp.dot(upper, sign_matrix, preferred_element_type=jnp.float32)
    total = total + jnp.dot(lower, sign_matrix, preferred_element_type=jnp.float32)
    return total * norm


def saturate(values):
    return jnp.clip(values, -saturation, saturation)


def fused_kernel(
    count,
    query_part,
    memory_part,
    out_weight_hbm,
    document_row,
    query_exponent,
    partial_exponent,
    summed_exponent,
    out_exponent,
    relevel,
    sign_ref,
    cosine_ref,
    sine_ref,
    out_ref,
    out_weight,
    first_near_send,
    first_near_recv,
    first_far_send,
    first_far_recv,
    memory_pair,
    mixed,
    second_near_send,
    second_near_recv,
    second_far_send,
    second_far_recv,
    total,
    weight_sem,
    near_send_sem,
    near_recv_sem,
    far_send_sem,
    far_recv_sem,
    pair_send_sem,
    pair_recv_sem,
):
    me = lax.axis_index("gx")
    core = lax.axis_index("gy")
    mate = 1 - core
    columns_of = count // 2
    column, row = me // 2, lax.rem(me, 2)
    neighbour = column * 2 + 1 - row
    length, width = query_part.shape[1], query_part.shape[2]
    span = out_ref.shape[2]
    blocks = span // width
    norm = 1.0 / math.sqrt(width)
    chunk = 2 * width
    mesh_ids = pl.DeviceIdType.MESH

    load = pltpu.make_async_copy(out_weight_hbm, out_weight, weight_sem)
    load.start()

    def column_at(step):
        return lax.rem(column + 1 + step, columns_of)

    barrier = pltpu.get_barrier_semaphore()
    pl.semaphore_signal(barrier, inc=1, device_id={"gy": mate}, device_id_type=mesh_ids)
    pl.semaphore_signal(barrier, inc=1, device_id={"gx": neighbour}, device_id_type=mesh_ids)
    for step in range(columns_of - 1):
        pl.semaphore_signal(
            barrier,
            inc=1,
            device_id={"gx": column_at(step) * 2 + row},
            device_id_type=mesh_ids,
        )
    pl.semaphore_wait(barrier, columns_of + 1)

    small_signs = sign_ref[:width, :width]

    def near_copy(send, recv, stage, step):
        return pltpu.make_async_remote_copy(
            src_ref=send.at[step],
            dst_ref=recv.at[step],
            send_sem=near_send_sem.at[stage, step],
            recv_sem=near_recv_sem.at[stage, step],
            device_id={"gx": neighbour},
            device_id_type=mesh_ids,
        )

    def far_copy(send, recv, stage, step):
        return pltpu.make_async_remote_copy(
            src_ref=send.at[step],
            dst_ref=recv.at[step],
            send_sem=far_send_sem.at[stage, step],
            recv_sem=far_recv_sem.at[stage, step],
            device_id={"gx": column_at(step) * 2 + row},
            device_id_type=mesh_ids,
        )

    def pair_copy(ref, place):
        return pltpu.make_async_remote_copy(
            src_ref=ref.at[core],
            dst_ref=ref.at[core],
            send_sem=pair_send_sem.at[place],
            recv_sem=pair_recv_sem.at[place],
            device_id={"gy": mate},
            device_id_type=mesh_ids,
        )

    def query_term(target):
        scale = power(-query_exponent[target, 0], width)
        return saturate(turn(query_part[target], small_signs, norm) * scale)

    def memory_term(target):
        scale = power(-partial_exponent[core, target], width)
        return saturate(turn(memory_part[core, target], small_signs, norm) * scale)

    def first_near(step, carry):
        target = column_at(step) * 2 + 1 - row
        first_near_send[step, 0] = query_term(target).astype(jnp.bfloat16)
        first_near_send[step, 1] = memory_term(target).astype(jnp.bfloat16)
        near_copy(first_near_send, first_near_recv, 0, step).start()
        return carry

    lax.fori_loop(0, columns_of, first_near, 0)

    def first_joined(step):
        target = column_at(step) * 2 + row
        query, memory = query_term(target), memory_term(target)
        near_copy(first_near_send, first_near_recv, 0, step).wait_recv()
        query = query + first_near_recv[step, 0].astype(jnp.float32)
        return query, memory + first_near_recv[step, 1].astype(jnp.float32)

    def first_far(step, carry):
        query, memory = first_joined(step)
        first_far_send[step, 0] = query.astype(jnp.bfloat16)
        first_far_send[step, 1] = memory.astype(jnp.bfloat16)
        far_copy(first_far_send, first_far_recv, 0, step).start()
        return carry

    lax.fori_loop(0, columns_of - 1, first_far, 0)
    query, memory = first_joined(columns_of - 1)
    total[:, :width] = query
    total[:, width : 2 * width] = memory

    def first_sum(step, carry):
        far_copy(first_far_send, first_far_recv, 0, step).wait_recv()
        total[:, :width] += first_far_recv[step, 0].astype(jnp.float32)
        total[:, width : 2 * width] += first_far_recv[step, 1].astype(jnp.float32)
        return carry

    lax.fori_loop(0, columns_of - 1, first_sum, 0)

    level_ratio = power(partial_exponent[core, me] - summed_exponent[core, me], width)
    level = saturate(total[:, width : 2 * width] * level_ratio)
    memory = turn(level * power(summed_exponent[core, me], width), small_signs, norm)
    turned = memory * cosine_ref[...] + pltpu.roll(memory, width // 2, 1) * sine_ref[...]
    memory_pair[core] = jnp.where(core == 0, turned, memory).astype(jnp.bfloat16)
    pair_copy(memory_pair, 0).start()
    query = turn(total[:, :width] * power(query_exponent[me, 0], width), small_signs, norm)
    query = query * cosine_ref[...] + pltpu.roll(query, width // 2, 1) * sine_ref[...]
    query = query.astype(jnp.bfloat16)
    rows = lax.broadcasted_iota(jnp.int32, (length, length), 0)
    columns = lax.broadcasted_iota(jnp.int32, (length, length), 1)
    documents = jnp.broadcast_to(document_row[...], (length, length)).astype(jnp.float32)
    allowed = (rows >= columns) & (documents.T == documents)
    pair_copy(memory_pair, 0).wait_recv()

    scores = lax.dot_general(
        query, memory_pair[0], (((1,), (1,)), ((), ())), preferred_element_type=jnp.float32
    ) * (1.0 / math.sqrt(width))
    scores = jnp.where(allowed, scores, -jnp.inf)
    exponentials = jnp.exp(scores - jnp.max(scores, axis=-1, keepdims=True))
    weights = exponentials / jnp.sum(exponentials, axis=-1, keepdims=True)
    mixed[core] = jnp.dot(
        weights.astype(jnp.bfloat16), memory_pair[1], preferred_element_type=jnp.float32
    ).astype(jnp.bfloat16)
    pair_copy(mixed, 1).start()
    load.wait()
    pair_copy(mixed, 1).wait_recv()

    def row_of(exponents):
        return jnp.concatenate([power(exponent, width) for exponent in exponents], axis=1)

    def second_term(target, part):
        start = pl.multiple_of(target * span + part * chunk, chunk)
        both = jnp.concatenate([mixed[0], mixed[1]], axis=1)
        product = jnp.dot(
            both, out_weight[:, pl.ds(start, chunk)], preferred_element_type=jnp.float32
        )
        block = target * blocks + part * 2
        scale = row_of([-out_exponent[0, block], -out_exponent[0, block + 1]])
        return saturate(turn(product, sign_ref[...], norm) * scale)

    places = [slice(part * chunk, (part + 1) * chunk) for part in range(span // chunk)]

    def second_near(step, carry):
        target = column_at(step) * 2 + 1 - row
        for part, place in enumerate(places):
            second_near_send[step, :, place] = second_term(target, part).astype(jnp.bfloat16)
        near_copy(second_near_send, second_near_recv, 1, step).start()
        return carry

    lax.fori_loop(0, columns_of, second_near, 0)

    def second_far(step, carry):
        near_copy(second_near_send, second_near_recv, 1, step).wait_recv()
        for part, place in enumerate(places):
            joined = second_term(column_at(step) * 2 + row, part)
            joined = joined + second_near_recv[step, :, place].astype(jnp.float32)
            second_far_send[step, :, place] = joined.astype(jnp.bfloat16)
        far_copy(second_far_send, second_far_recv, 1, step).start()
        return carry

    lax.fori_loop(0, columns_of - 1, second_far, 0)
    last = columns_of - 1
    for part, place in enumerate(places):
        total[:, place] = second_term(me, part)
    near_copy(second_near_send, second_near_recv, 1, last).wait_recv()
    for place in places:
        total[:, place] += second_near_recv[last, :, place].astype(jnp.float32)

    def second_sum(step, carry):
        far_copy(second_far_send, second_far_recv, 1, step).wait_recv()
        for place in places:
            total[:, place] += second_far_recv[step, :, place].astype(jnp.float32)
        return carry

    lax.fori_loop(0, columns_of - 1, second_sum, 0)
    for part, place in enumerate(places):
        summed = [out_exponent[0, me * blocks + part * 2 + i] for i in range(2)]
        ending = [relevel[core, part * 2 + i] for i in range(2)]
        ratio = row_of([start - end for start, end in zip(summed, ending)])
        level = saturate(total[:, place] * ratio) * row_of(ending)
        out_ref[core, :, place] = turn(level, sign_ref[...], norm).astype(jnp.bfloat16)
    pair_copy(out_ref, 2).start()

    def drain_near(step, carry):
        near_copy(first_near_send, first_near_recv, 0, step).wait_send()
        near_copy(second_near_send, second_near_recv, 1, step).wait_send()
        return carry

    def drain_far(step, carry):
        far_copy(first_far_send, first_far_recv, 0, step).wait_send()
        far_copy(second_far_send, second_far_recv, 1, step).wait_send()
        return carry

    lax.fori_loop(0, columns_of, drain_near, 0)
    lax.fori_loop(0, columns_of - 1, drain_far, 0)
    pair_copy(memory_pair, 0).wait_send()
    pair_copy(mixed, 1).wait_send()
    pair_copy(out_ref, 2).wait()


def body(
    tokens,
    query_weight,
    key_value_projection_weight,
    output_weight,
    document_ids,
    query_exponent,
    key_value_partial_exponents,
    key_value_summed_exponents,
    output_exponent,
    output_relevel,
):
    count = lax.axis_size("gx")
    length = tokens.shape[0]
    width = query_weight.shape[3]
    heads = query_weight.shape[1]
    memory_heads = key_value_projection_weight.shape[2]
    span = output_weight.shape[1] // count
    even = count % 2 == 0 and lax.axis_size("gy") == 2 and span % (2 * width) == 0
    if not (even and count == heads == memory_heads):
        return plain_body(
            tokens,
            query_weight,
            key_value_projection_weight,
            output_weight,
            document_ids,
            query_exponent,
            key_value_partial_exponents,
            key_value_summed_exponents,
            output_exponent,
            output_relevel,
        )
    query_part = jnp.einsum(
        "sd,dpe->pse", tokens, query_weight[:, :, 0, :], preferred_element_type=jnp.float32
    )
    memory_part = jnp.einsum(
        "sd,dcne->cnse", tokens, key_value_projection_weight, preferred_element_type=jnp.float32
    )
    cosine, sine = rotary_tables(length, width)
    vmem = pl.BlockSpec(memory_space=pltpu.VMEM)
    smem = pl.BlockSpec(memory_space=pltpu.SMEM)
    half = count // 2
    bf16 = jnp.bfloat16
    halves = pl.pallas_call(
        functools.partial(fused_kernel, count),
        out_shape=jax.ShapeDtypeStruct((2, length, span), bf16),
        in_specs=[vmem, vmem, pl.BlockSpec(memory_space=pl.ANY), vmem] + [smem] * 5 + [vmem] * 3,
        out_specs=vmem,
        scratch_shapes=[
            pltpu.VMEM(output_weight.shape, bf16),
            pltpu.VMEM((half, 2, length, width), bf16),
            pltpu.VMEM((half, 2, length, width), bf16),
            pltpu.VMEM((half - 1, 2, length, width), bf16),
            pltpu.VMEM((half - 1, 2, length, width), bf16),
            pltpu.VMEM((2, length, width), bf16),
            pltpu.VMEM((2, length, width), bf16),
            pltpu.VMEM((half, length, span), bf16),
            pltpu.VMEM((half, length, span), bf16),
            pltpu.VMEM((half - 1, length, span), bf16),
            pltpu.VMEM((half - 1, length, span), bf16),
            pltpu.VMEM((length, span), jnp.float32),
            pltpu.SemaphoreType.DMA,
            pltpu.SemaphoreType.DMA((2, half)),
            pltpu.SemaphoreType.DMA((2, half)),
            pltpu.SemaphoreType.DMA((2, half - 1)),
            pltpu.SemaphoreType.DMA((2, half - 1)),
            pltpu.SemaphoreType.DMA((3,)),
            pltpu.SemaphoreType.DMA((3,)),
        ],
        compiler_params=pltpu.CompilerParams(
            collective_id=0, has_side_effects=True, vmem_limit_bytes=40 * 1024 * 1024
        ),
    )(
        query_part,
        memory_part,
        output_weight,
        document_ids[None, :],
        query_exponent,
        key_value_partial_exponents,
        key_value_summed_exponents,
        output_exponent,
        output_relevel,
        jnp.asarray(paired_signs(width), bf16),
        jnp.asarray(cosine),
        jnp.asarray(sine),
    )
    return halves.transpose(1, 0, 2)


def solution(mesh):
    return jax.shard_map(
        body,
        mesh=mesh,
        in_specs=(
            P("groups", "gx"),
            P("gx", None, "gy", None),
            P("gx", None, None, None),
            P("gx", "gy"),
            P("groups"),
            P(None, "gy"),
            P(),
            P(),
            P("gy", None),
            P(None, "gx"),
        ),
        out_specs=P("groups", None, "gx"),
        check_vma=False,
    )
```

```python
import functools
import math

import jax
import jax.numpy as jnp
import numpy as np
from jax import lax
from jax.experimental import pallas as pl
from jax.experimental.pallas import tpu as pltpu
from jax.sharding import PartitionSpec as P

rotary_base = 500000.0
saturation = 127.0


def hadamard(order):
    row_index = jnp.arange(order, dtype=jnp.int32)[:, None]
    col_index = jnp.arange(order, dtype=jnp.int32)[None, :]
    common = row_index & col_index
    parity = jnp.zeros((order, order), jnp.int32)
    for bit_place in range(order.bit_length() - 1):
        parity = parity ^ common >> bit_place & 1
    return (1 - 2 * parity).astype(jnp.float32) * (1.0 / math.sqrt(order))


def rotate(values, rotation):
    return jnp.matmul(values, rotation, precision=lax.Precision.HIGHEST)


def rotary(values):
    length = values.shape[-2]
    full_width = values.shape[-1]
    half_width = full_width // 2
    frequency = rotary_base ** (-(jnp.arange(half_width, dtype=jnp.float32) * 2.0 / full_width))
    places = jnp.arange(length, dtype=jnp.int32).astype(jnp.float32)
    angles = places[:, None] * frequency[None, :]
    cosine = jnp.cos(angles)
    sine_part = jnp.sin(angles)
    front_half = values[..., :half_width]
    back_half = values[..., half_width:]
    return jnp.concatenate(
        [front_half * cosine - back_half * sine_part, back_half * cosine + front_half * sine_part],
        axis=-1,
    )


def plain_body(
    tokens,
    query_weight,
    key_value_projection_weight,
    output_weight,
    document_ids,
    query_exponent,
    key_value_partial_exponents,
    key_value_summed_exponents,
    output_exponent,
    output_relevel,
):
    length = tokens.shape[0]
    head_width = query_weight.shape[3]
    memory_heads = key_value_projection_weight.shape[2]
    count_gx = lax.axis_size("gx")
    where_gx = lax.axis_index("gx")
    where_gy = lax.axis_index("gy")
    rotation = hadamard(head_width)
    query_block = query_weight[:, :, 0, :]
    query_inverse = jnp.exp2(-query_exponent[:, 0].astype(jnp.float32))
    query_up = jnp.exp2(query_exponent[:, 0].astype(jnp.float32))
    heads_total = query_block.shape[1]
    heads_here = heads_total // count_gx
    heads_spread = count_gx // memory_heads
    memory_index = where_gx // heads_spread
    memory_inverse = jnp.exp2(-key_value_partial_exponents.astype(jnp.float32))
    memory_up = jnp.exp2(key_value_partial_exponents.astype(jnp.float32))
    memory_scale = jnp.exp2(key_value_summed_exponents.astype(jnp.float32))
    partial_sum = jnp.einsum("sd,dpe->pse", tokens, query_block, preferred_element_type=jnp.float32)
    factor = query_inverse
    query_sum = lax.psum_scatter(
        jnp.clip(rotate(partial_sum, rotation) * factor[:, None, None], -saturation, saturation),
        "gx",
        scatter_dimension=0,
        tiled=True,
    )
    query_scale = lax.dynamic_slice_in_dim(query_up, where_gx * heads_here, heads_here, 0)
    query = rotary(rotate(query_sum * query_scale[:, None, None], rotation))[0].astype(jnp.bfloat16)
    partial_sum = jnp.einsum(
        "sd,dche->sche", tokens, key_value_projection_weight, preferred_element_type=jnp.float32
    )
    memory_sum = lax.psum_scatter(
        jnp.clip(
            rotate(partial_sum, rotation) * memory_inverse[None, :, :, None],
            -saturation,
            saturation,
        ),
        "gx",
        scatter_dimension=0,
        tiled=True,
    )
    whole = lax.all_gather(
        jnp.clip(
            memory_sum * memory_up[None, :, :, None] / memory_scale[None, :, :, None],
            -saturation,
            saturation,
        ),
        "gx",
        axis=0,
        tiled=True,
    )
    arrived = lax.dynamic_index_in_dim(whole, memory_index, 2, keepdims=False)
    head_scale = lax.dynamic_index_in_dim(memory_scale, memory_index, 1, keepdims=False)
    memory_full = rotate(arrived * head_scale[None, :, None], rotation)
    keys = rotary(memory_full[:, 0]).astype(jnp.bfloat16)
    values = memory_full[:, 1].astype(jnp.bfloat16)
    scores = jnp.einsum("qe,ke->qk", query, keys, preferred_element_type=jnp.float32) * (
        1.0 / math.sqrt(head_width)
    )
    position = jnp.arange(length, dtype=jnp.int32)
    allowed = (position[:, None] >= position[None, :]) & (
        document_ids[:, None] == document_ids[None, :]
    )
    scores = jnp.where(allowed, scores, -jnp.inf)
    row_max = jnp.max(scores, axis=-1, keepdims=True)
    exponentials = jnp.exp(scores - row_max)
    weights = (exponentials / jnp.sum(exponentials, axis=-1, keepdims=True)).astype(jnp.bfloat16)
    attended = jnp.dot(weights, values, preferred_element_type=jnp.float32).astype(jnp.bfloat16)
    head_pairs = lax.all_gather(attended, "gy", axis=1, tiled=True)
    feature_blocks = output_weight.shape[1] // head_width
    blocks_here = feature_blocks // count_gx
    output_inverse = jnp.exp2(-output_exponent[0].astype(jnp.float32))
    partial_sum = jnp.dot(head_pairs, output_weight, preferred_element_type=jnp.float32)
    partial_sum = partial_sum.reshape(
        length, blocks_here * lax.axis_size("gx"), head_width
    ).transpose(1, 0, 2)
    factor = output_inverse
    out_sum = lax.psum_scatter(
        jnp.clip(rotate(partial_sum, rotation) * factor[:, None, None], -saturation, saturation),
        "gx",
        scatter_dimension=0,
        tiled=True,
    )
    out_up = jnp.exp2(
        lax.dynamic_slice_in_dim(output_exponent[0], where_gx * blocks_here, blocks_here, 0).astype(
            jnp.float32
        )
    )
    own_scale = jnp.exp2(
        lax.dynamic_index_in_dim(output_relevel, where_gy, 0, keepdims=False).astype(jnp.float32)
    )
    out_level = jnp.clip(
        out_sum * out_up[:, None, None] / own_scale[:, None, None], -saturation, saturation
    )
    halves = lax.all_gather(out_level[None], "gy", axis=0, tiled=True)
    restored = rotate(
        halves * jnp.exp2(output_relevel.astype(jnp.float32))[:, :, None, None], rotation
    )
    return (
        restored.transpose(2, 0, 1, 3)
        .reshape(length, 2, blocks_here * head_width)
        .astype(jnp.bfloat16)
    )


def signs(order):
    index = np.arange(order)
    common = index[:, None] & index[None, :]
    parity = np.zeros((order, order), np.int64)
    for place in range(order.bit_length() - 1):
        parity ^= (common >> place) & 1
    return 1.0 - 2.0 * parity


def paired_signs(order):
    return np.kron(np.eye(2), signs(order))


def rotary_tables(length, width):
    half = width // 2
    frequency = rotary_base ** (-(np.arange(half, dtype=np.float64) * 2.0 / width))
    angles = np.arange(length)[:, None] * frequency.astype(np.float32).astype(np.float64)[None, :]
    cosine = np.concatenate([np.cos(angles), np.cos(angles)], axis=1)
    sine = np.concatenate([-np.sin(angles), np.sin(angles)], axis=1)
    return cosine.astype(np.float32), sine.astype(np.float32)


def power(exponent, width):
    row = jnp.full((1, width), exponent, jnp.int32)
    size = jnp.abs(row)
    upward = jnp.ones((1, width), jnp.float32)
    downward = jnp.ones((1, width), jnp.float32)
    for place in (1, 2, 4, 8, 16):
        taken = (size & place) != 0
        upward = jnp.where(taken, upward * 2.0**place, upward)
        downward = jnp.where(taken, downward * 2.0**-place, downward)
    return jnp.where(row >= 0, upward, downward)


def turn(values, sign_matrix, norm):
    upper = values.astype(jnp.bfloat16)
    lower = (values - upper.astype(jnp.float32)).astype(jnp.bfloat16)
    total = jnp.dot(upper, sign_matrix, preferred_element_type=jnp.float32)
    total = total + jnp.dot(lower, sign_matrix, preferred_element_type=jnp.float32)
    return total * norm


def saturate(values):
    return jnp.clip(values, -saturation, saturation)


def fused_kernel(
    count,
    query_part,
    memory_part,
    out_weight_hbm,
    document_row,
    query_exponent,
    partial_exponent,
    summed_exponent,
    out_exponent,
    relevel,
    sign_ref,
    cosine_ref,
    sine_ref,
    out_ref,
    out_weight,
    first_near_send,
    first_near_recv,
    first_far_send,
    first_far_recv,
    memory_pair,
    mixed,
    second_near_send,
    second_near_recv,
    second_far_send,
    second_far_recv,
    first_total,
    total,
    bias,
    weight_sem,
    near_send_sem,
    near_recv_sem,
    far_send_sem,
    far_recv_sem,
    pair_send_sem,
    pair_recv_sem,
    piece_near_send,
    piece_near_recv,
    piece_far_send,
    piece_far_recv,
    out_send_sem,
    out_recv_sem,
):
    me = lax.axis_index("gx")
    core = lax.axis_index("gy")
    mate = 1 - core
    columns_of = count // 2
    column, row = me // 2, lax.rem(me, 2)
    neighbour = column * 2 + 1 - row
    length, width = query_part.shape[1], query_part.shape[2]
    span = out_ref.shape[2]
    blocks = span // width
    norm = 1.0 / math.sqrt(width)
    chunk = 2 * width
    mesh_ids = pl.DeviceIdType.MESH

    load = pltpu.make_async_copy(out_weight_hbm, out_weight, weight_sem)
    load.start()

    def column_at(step):
        return lax.rem(column + 1 + step, columns_of)

    barrier = pltpu.get_barrier_semaphore()
    pl.semaphore_signal(barrier, inc=1, device_id={"gy": mate}, device_id_type=mesh_ids)
    pl.semaphore_signal(barrier, inc=1, device_id={"gx": neighbour}, device_id_type=mesh_ids)
    for step in range(columns_of - 1):
        pl.semaphore_signal(
            barrier,
            inc=1,
            device_id={"gx": column_at(step) * 2 + row},
            device_id_type=mesh_ids,
        )
    pl.semaphore_wait(barrier, columns_of + 1)

    small_signs = sign_ref[:width, :width]

    def near_copy(send, recv, stage, step):
        return pltpu.make_async_remote_copy(
            src_ref=send.at[step],
            dst_ref=recv.at[step],
            send_sem=near_send_sem.at[stage, step],
            recv_sem=near_recv_sem.at[stage, step],
            device_id={"gx": neighbour},
            device_id_type=mesh_ids,
        )

    def far_copy(send, recv, stage, step):
        return pltpu.make_async_remote_copy(
            src_ref=send.at[step],
            dst_ref=recv.at[step],
            send_sem=far_send_sem.at[stage, step],
            recv_sem=far_recv_sem.at[stage, step],
            device_id={"gx": column_at(step) * 2 + row},
            device_id_type=mesh_ids,
        )

    def pair_copy(ref, place):
        return pltpu.make_async_remote_copy(
            src_ref=ref.at[core],
            dst_ref=ref.at[core],
            send_sem=pair_send_sem.at[place],
            recv_sem=pair_recv_sem.at[place],
            device_id={"gy": mate},
            device_id_type=mesh_ids,
        )

    def query_term(target):
        scale = power(-query_exponent[target, 0], width)
        return saturate(turn(query_part[target], small_signs, norm) * scale)

    def memory_term(target):
        scale = power(-partial_exponent[core, target], width)
        return saturate(turn(memory_part[core, target], small_signs, norm) * scale)

    def first_near(step, carry):
        target = column_at(step) * 2 + 1 - row
        first_near_send[step, 0] = query_term(target).astype(jnp.bfloat16)
        first_near_send[step, 1] = memory_term(target).astype(jnp.bfloat16)
        near_copy(first_near_send, first_near_recv, 0, step).start()
        return carry

    lax.fori_loop(0, columns_of, first_near, 0)

    def first_joined(step):
        target = column_at(step) * 2 + row
        query, memory = query_term(target), memory_term(target)
        near_copy(first_near_send, first_near_recv, 0, step).wait_recv()
        query = query + first_near_recv[step, 0].astype(jnp.float32)
        return query, memory + first_near_recv[step, 1].astype(jnp.float32)

    def first_far(step, carry):
        query, memory = first_joined(step)
        first_far_send[step, 0] = query.astype(jnp.bfloat16)
        first_far_send[step, 1] = memory.astype(jnp.bfloat16)
        far_copy(first_far_send, first_far_recv, 0, step).start()
        return carry

    lax.fori_loop(0, columns_of - 1, first_far, 0)
    query, memory = first_joined(columns_of - 1)
    first_total[0] = query
    first_total[1] = memory

    rows = lax.broadcasted_iota(jnp.int32, (length, length), 0)
    columns = lax.broadcasted_iota(jnp.int32, (length, length), 1)
    documents = jnp.broadcast_to(document_row[...], (length, length)).astype(jnp.float32)
    allowed = (rows >= columns) & (documents.T == documents)
    bias[...] = jnp.where(allowed, 0.0, -jnp.inf)

    def first_sum(step, carry):
        far_copy(first_far_send, first_far_recv, 0, step).wait_recv()
        first_total[0] += first_far_recv[step, 0].astype(jnp.float32)
        first_total[1] += first_far_recv[step, 1].astype(jnp.float32)
        return carry

    lax.fori_loop(0, columns_of - 1, first_sum, 0)

    level_ratio = power(partial_exponent[core, me] - summed_exponent[core, me], width)
    level = saturate(first_total[1] * level_ratio)
    memory = turn(level * power(summed_exponent[core, me], width), small_signs, norm)
    turned = memory * cosine_ref[...] + pltpu.roll(memory, width // 2, 1) * sine_ref[...]
    memory_pair[core] = jnp.where(core == 0, turned, memory).astype(jnp.bfloat16)
    pair_copy(memory_pair, 0).start()
    query = turn(first_total[0] * power(query_exponent[me, 0], width), small_signs, norm)
    query = query * cosine_ref[...] + pltpu.roll(query, width // 2, 1) * sine_ref[...]
    query = query.astype(jnp.bfloat16)
    pair_copy(memory_pair, 0).wait_recv()

    scores = lax.dot_general(
        query, memory_pair[0], (((1,), (1,)), ((), ())), preferred_element_type=jnp.float32
    ) * (1.0 / math.sqrt(width))
    scores = scores + bias[...]
    exponentials = jnp.exp(scores - jnp.max(scores, axis=-1, keepdims=True))
    weights = exponentials / jnp.sum(exponentials, axis=-1, keepdims=True)
    mixed[core] = jnp.dot(
        weights.astype(jnp.bfloat16), memory_pair[1], preferred_element_type=jnp.float32
    ).astype(jnp.bfloat16)
    pair_copy(mixed, 1).start()
    load.wait()
    pair_copy(mixed, 1).wait_recv()

    def row_of(exponents):
        return jnp.concatenate([power(exponent, width) for exponent in exponents], axis=1)

    def second_term(target, part):
        start = pl.multiple_of((target * (span // chunk) + part) * chunk, chunk)
        both = jnp.concatenate([mixed[0], mixed[1]], axis=1)
        product = jnp.dot(
            both, out_weight[:, pl.ds(start, chunk)], preferred_element_type=jnp.float32
        )
        block = target * blocks + part * 2
        scale = row_of([-out_exponent[0, block], -out_exponent[0, block + 1]])
        return saturate(turn(product, sign_ref[...], norm) * scale)

    parts = span // chunk
    ahead = min(3, parts)
    near_total, far_total = columns_of * parts, (columns_of - 1) * parts

    def piece_copy(kind, piece):
        send, recv, send_sem, recv_sem, target = {
            "near": (second_near_send, second_near_recv, piece_near_send, piece_near_recv, None),
            "far": (second_far_send, second_far_recv, piece_far_send, piece_far_recv, 1),
        }[kind]
        if target is None:
            target = neighbour
        else:
            target = column_at(piece // parts) * 2 + row
        return pltpu.make_async_remote_copy(
            src_ref=send.at[piece],
            dst_ref=recv.at[piece],
            send_sem=send_sem.at[piece],
            recv_sem=recv_sem.at[piece],
            device_id={"gx": target},
            device_id_type=mesh_ids,
        )

    def second_near(piece, carry):
        target = column_at(piece // parts) * 2 + 1 - row
        second_near_send[piece] = second_term(target, piece % parts).astype(jnp.bfloat16)
        piece_copy("near", piece).start()
        return carry

    def second_joined(piece):
        term = second_term(column_at(piece // parts) * 2 + row, piece % parts)
        piece_copy("near", piece).wait_recv()
        return term + second_near_recv[piece].astype(jnp.float32)

    def second_far(piece, carry):
        second_near(piece + ahead, 0)
        second_far_send[piece] = second_joined(piece).astype(jnp.bfloat16)
        piece_copy("far", piece).start()
        return carry

    lax.fori_loop(0, ahead, second_near, 0)
    lax.fori_loop(0, far_total, second_far, 0)
    lax.fori_loop(far_total + ahead, near_total, second_near, 0)

    def second_own(part, carry):
        total[part] = second_joined(far_total + part)
        return carry

    lax.fori_loop(0, parts, second_own, 0)

    def second_sum(piece, carry):
        piece_copy("far", piece).wait_recv()
        total[piece % parts] += second_far_recv[piece].astype(jnp.float32)
        return carry

    lax.fori_loop(0, far_total - parts, second_sum, 0)

    def out_copy(part):
        place = slice(part * chunk, (part + 1) * chunk)
        return pltpu.make_async_remote_copy(
            src_ref=out_ref.at[core, :, place],
            dst_ref=out_ref.at[core, :, place],
            send_sem=out_send_sem.at[part],
            recv_sem=out_recv_sem.at[part],
            device_id={"gy": mate},
            device_id_type=mesh_ids,
        )

    for part in range(parts):
        second_sum(far_total - parts + part, 0)
        summed = [out_exponent[0, me * blocks + part * 2 + i] for i in range(2)]
        ending = [relevel[core, part * 2 + i] for i in range(2)]
        ratio = row_of([start - end for start, end in zip(summed, ending)])
        level = saturate(total[part] * ratio) * row_of(ending)
        out_ref[core, :, part * chunk : (part + 1) * chunk] = turn(
            level, sign_ref[...], norm
        ).astype(jnp.bfloat16)
        out_copy(part).start()

    def drain_near(step, carry):
        near_copy(first_near_send, first_near_recv, 0, step).wait_send()
        return carry

    def drain_far(step, carry):
        far_copy(first_far_send, first_far_recv, 0, step).wait_send()
        return carry

    def drain_near_piece(piece, carry):
        piece_copy("near", piece).wait_send()
        return carry

    def drain_far_piece(piece, carry):
        piece_copy("far", piece).wait_send()
        return carry

    lax.fori_loop(0, near_total, drain_near_piece, 0)
    lax.fori_loop(0, far_total, drain_far_piece, 0)
    lax.fori_loop(0, columns_of, drain_near, 0)
    lax.fori_loop(0, columns_of - 1, drain_far, 0)
    pair_copy(memory_pair, 0).wait_send()
    pair_copy(mixed, 1).wait_send()
    for part in range(parts):
        out_copy(part).wait()


def body(
    tokens,
    query_weight,
    key_value_projection_weight,
    output_weight,
    document_ids,
    query_exponent,
    key_value_partial_exponents,
    key_value_summed_exponents,
    output_exponent,
    output_relevel,
):
    count = lax.axis_size("gx")
    length = tokens.shape[0]
    width = query_weight.shape[3]
    heads = query_weight.shape[1]
    memory_heads = key_value_projection_weight.shape[2]
    span = output_weight.shape[1] // count
    even = count % 2 == 0 and lax.axis_size("gy") == 2 and span % (2 * width) == 0
    if not (even and count == heads == memory_heads):
        return plain_body(
            tokens,
            query_weight,
            key_value_projection_weight,
            output_weight,
            document_ids,
            query_exponent,
            key_value_partial_exponents,
            key_value_summed_exponents,
            output_exponent,
            output_relevel,
        )
    query_part = jnp.einsum(
        "sd,dpe->pse", tokens, query_weight[:, :, 0, :], preferred_element_type=jnp.float32
    )
    memory_part = jnp.einsum(
        "sd,dcne->cnse", tokens, key_value_projection_weight, preferred_element_type=jnp.float32
    )
    cosine, sine = rotary_tables(length, width)
    vmem = pl.BlockSpec(memory_space=pltpu.VMEM)
    smem = pl.BlockSpec(memory_space=pltpu.SMEM)
    half = count // 2
    parts = span // (2 * width)
    bf16 = jnp.bfloat16
    halves = pl.pallas_call(
        functools.partial(fused_kernel, count),
        out_shape=jax.ShapeDtypeStruct((2, length, span), bf16),
        in_specs=[vmem, vmem, pl.BlockSpec(memory_space=pl.ANY), vmem] + [smem] * 5 + [vmem] * 3,
        out_specs=vmem,
        scratch_shapes=[
            pltpu.VMEM(output_weight.shape, bf16),
            pltpu.VMEM((half, 2, length, width), bf16),
            pltpu.VMEM((half, 2, length, width), bf16),
            pltpu.VMEM((half - 1, 2, length, width), bf16),
            pltpu.VMEM((half - 1, 2, length, width), bf16),
            pltpu.VMEM((2, length, width), bf16),
            pltpu.VMEM((2, length, width), bf16),
            pltpu.VMEM((half * parts, length, 2 * width), bf16),
            pltpu.VMEM((half * parts, length, 2 * width), bf16),
            pltpu.VMEM(((half - 1) * parts, length, 2 * width), bf16),
            pltpu.VMEM(((half - 1) * parts, length, 2 * width), bf16),
            pltpu.VMEM((2, length, width), jnp.float32),
            pltpu.VMEM((parts, length, 2 * width), jnp.float32),
            pltpu.VMEM((length, length), jnp.float32),
            pltpu.SemaphoreType.DMA,
            pltpu.SemaphoreType.DMA((1, half)),
            pltpu.SemaphoreType.DMA((1, half)),
            pltpu.SemaphoreType.DMA((1, half - 1)),
            pltpu.SemaphoreType.DMA((1, half - 1)),
            pltpu.SemaphoreType.DMA((2,)),
            pltpu.SemaphoreType.DMA((2,)),
            pltpu.SemaphoreType.DMA((half * parts,)),
            pltpu.SemaphoreType.DMA((half * parts,)),
            pltpu.SemaphoreType.DMA(((half - 1) * parts,)),
            pltpu.SemaphoreType.DMA(((half - 1) * parts,)),
            pltpu.SemaphoreType.DMA((parts,)),
            pltpu.SemaphoreType.DMA((parts,)),
        ],
        compiler_params=pltpu.CompilerParams(
            collective_id=0, has_side_effects=True, vmem_limit_bytes=40 * 1024 * 1024
        ),
    )(
        query_part,
        memory_part,
        output_weight,
        document_ids[None, :],
        query_exponent,
        key_value_partial_exponents,
        key_value_summed_exponents,
        output_exponent,
        output_relevel,
        jnp.asarray(paired_signs(width), bf16),
        jnp.asarray(cosine),
        jnp.asarray(sine),
    )
    return halves.transpose(1, 0, 2)


def solution(mesh):
    return jax.shard_map(
        body,
        mesh=mesh,
        in_specs=(
            P("groups", "gx"),
            P("gx", None, "gy", None),
            P("gx", None, None, None),
            P("gx", "gy"),
            P("groups"),
            P(None, "gy"),
            P(),
            P(),
            P("gy", None),
            P(None, "gx"),
        ),
        out_specs=P("groups", None, "gx"),
        check_vma=False,
    )
```

```python
import functools
import math

import jax
import jax.numpy as jnp
import numpy as np
from jax import lax
from jax.experimental import pallas as pl
from jax.experimental.pallas import tpu as pltpu
from jax.sharding import PartitionSpec as P

rotary_base = 500000.0
saturation = 127.0


def hadamard(order):
    row_index = jnp.arange(order, dtype=jnp.int32)[:, None]
    col_index = jnp.arange(order, dtype=jnp.int32)[None, :]
    common = row_index & col_index
    parity = jnp.zeros((order, order), jnp.int32)
    for bit_place in range(order.bit_length() - 1):
        parity = parity ^ common >> bit_place & 1
    return (1 - 2 * parity).astype(jnp.float32) * (1.0 / math.sqrt(order))


def rotate(values, rotation):
    return jnp.matmul(values, rotation, precision=lax.Precision.HIGHEST)


def rotary(values):
    length = values.shape[-2]
    full_width = values.shape[-1]
    half_width = full_width // 2
    frequency = rotary_base ** (-(jnp.arange(half_width, dtype=jnp.float32) * 2.0 / full_width))
    places = jnp.arange(length, dtype=jnp.int32).astype(jnp.float32)
    angles = places[:, None] * frequency[None, :]
    cosine = jnp.cos(angles)
    sine_part = jnp.sin(angles)
    front_half = values[..., :half_width]
    back_half = values[..., half_width:]
    return jnp.concatenate(
        [front_half * cosine - back_half * sine_part, back_half * cosine + front_half * sine_part],
        axis=-1,
    )


def plain_body(
    tokens,
    query_weight,
    key_value_projection_weight,
    output_weight,
    document_ids,
    query_exponent,
    key_value_partial_exponents,
    key_value_summed_exponents,
    output_exponent,
    output_relevel,
):
    length = tokens.shape[0]
    head_width = query_weight.shape[3]
    memory_heads = key_value_projection_weight.shape[2]
    count_gx = lax.axis_size("gx")
    where_gx = lax.axis_index("gx")
    where_gy = lax.axis_index("gy")
    rotation = hadamard(head_width)
    query_block = query_weight[:, :, 0, :]
    query_inverse = jnp.exp2(-query_exponent[:, 0].astype(jnp.float32))
    query_up = jnp.exp2(query_exponent[:, 0].astype(jnp.float32))
    heads_total = query_block.shape[1]
    heads_here = heads_total // count_gx
    heads_spread = count_gx // memory_heads
    memory_index = where_gx // heads_spread
    memory_inverse = jnp.exp2(-key_value_partial_exponents.astype(jnp.float32))
    memory_up = jnp.exp2(key_value_partial_exponents.astype(jnp.float32))
    memory_scale = jnp.exp2(key_value_summed_exponents.astype(jnp.float32))
    partial_sum = jnp.einsum("sd,dpe->pse", tokens, query_block, preferred_element_type=jnp.float32)
    factor = query_inverse
    query_sum = lax.psum_scatter(
        jnp.clip(rotate(partial_sum, rotation) * factor[:, None, None], -saturation, saturation),
        "gx",
        scatter_dimension=0,
        tiled=True,
    )
    query_scale = lax.dynamic_slice_in_dim(query_up, where_gx * heads_here, heads_here, 0)
    query = rotary(rotate(query_sum * query_scale[:, None, None], rotation))[0].astype(jnp.bfloat16)
    partial_sum = jnp.einsum(
        "sd,dche->sche", tokens, key_value_projection_weight, preferred_element_type=jnp.float32
    )
    memory_sum = lax.psum_scatter(
        jnp.clip(
            rotate(partial_sum, rotation) * memory_inverse[None, :, :, None],
            -saturation,
            saturation,
        ),
        "gx",
        scatter_dimension=0,
        tiled=True,
    )
    whole = lax.all_gather(
        jnp.clip(
            memory_sum * memory_up[None, :, :, None] / memory_scale[None, :, :, None],
            -saturation,
            saturation,
        ),
        "gx",
        axis=0,
        tiled=True,
    )
    arrived = lax.dynamic_index_in_dim(whole, memory_index, 2, keepdims=False)
    head_scale = lax.dynamic_index_in_dim(memory_scale, memory_index, 1, keepdims=False)
    memory_full = rotate(arrived * head_scale[None, :, None], rotation)
    keys = rotary(memory_full[:, 0]).astype(jnp.bfloat16)
    values = memory_full[:, 1].astype(jnp.bfloat16)
    scores = jnp.einsum("qe,ke->qk", query, keys, preferred_element_type=jnp.float32) * (
        1.0 / math.sqrt(head_width)
    )
    position = jnp.arange(length, dtype=jnp.int32)
    allowed = (position[:, None] >= position[None, :]) & (
        document_ids[:, None] == document_ids[None, :]
    )
    scores = jnp.where(allowed, scores, -jnp.inf)
    row_max = jnp.max(scores, axis=-1, keepdims=True)
    exponentials = jnp.exp(scores - row_max)
    weights = (exponentials / jnp.sum(exponentials, axis=-1, keepdims=True)).astype(jnp.bfloat16)
    attended = jnp.dot(weights, values, preferred_element_type=jnp.float32).astype(jnp.bfloat16)
    head_pairs = lax.all_gather(attended, "gy", axis=1, tiled=True)
    feature_blocks = output_weight.shape[1] // head_width
    blocks_here = feature_blocks // count_gx
    output_inverse = jnp.exp2(-output_exponent[0].astype(jnp.float32))
    partial_sum = jnp.dot(head_pairs, output_weight, preferred_element_type=jnp.float32)
    partial_sum = partial_sum.reshape(
        length, blocks_here * lax.axis_size("gx"), head_width
    ).transpose(1, 0, 2)
    factor = output_inverse
    out_sum = lax.psum_scatter(
        jnp.clip(rotate(partial_sum, rotation) * factor[:, None, None], -saturation, saturation),
        "gx",
        scatter_dimension=0,
        tiled=True,
    )
    out_up = jnp.exp2(
        lax.dynamic_slice_in_dim(output_exponent[0], where_gx * blocks_here, blocks_here, 0).astype(
            jnp.float32
        )
    )
    own_scale = jnp.exp2(
        lax.dynamic_index_in_dim(output_relevel, where_gy, 0, keepdims=False).astype(jnp.float32)
    )
    out_level = jnp.clip(
        out_sum * out_up[:, None, None] / own_scale[:, None, None], -saturation, saturation
    )
    halves = lax.all_gather(out_level[None], "gy", axis=0, tiled=True)
    restored = rotate(
        halves * jnp.exp2(output_relevel.astype(jnp.float32))[:, :, None, None], rotation
    )
    return (
        restored.transpose(2, 0, 1, 3)
        .reshape(length, 2, blocks_here * head_width)
        .astype(jnp.bfloat16)
    )


def signs(order):
    index = np.arange(order)
    common = index[:, None] & index[None, :]
    parity = np.zeros((order, order), np.int64)
    for place in range(order.bit_length() - 1):
        parity ^= (common >> place) & 1
    return 1.0 - 2.0 * parity


def paired_signs(order):
    return np.kron(np.eye(2), signs(order))


def rotary_tables(length, width):
    half = width // 2
    frequency = rotary_base ** (-(np.arange(half, dtype=np.float64) * 2.0 / width))
    angles = np.arange(length)[:, None] * frequency.astype(np.float32).astype(np.float64)[None, :]
    cosine = np.concatenate([np.cos(angles), np.cos(angles)], axis=1)
    sine = np.concatenate([-np.sin(angles), np.sin(angles)], axis=1)
    return cosine.astype(np.float32), sine.astype(np.float32)


def power(exponent, width):
    row = jnp.full((1, width), exponent, jnp.int32)
    size = jnp.abs(row)
    upward = jnp.ones((1, width), jnp.float32)
    downward = jnp.ones((1, width), jnp.float32)
    for place in (1, 2, 4, 8, 16):
        taken = (size & place) != 0
        upward = jnp.where(taken, upward * 2.0**place, upward)
        downward = jnp.where(taken, downward * 2.0**-place, downward)
    return jnp.where(row >= 0, upward, downward)


def turn(values, sign_matrix, norm):
    upper = values.astype(jnp.bfloat16)
    lower = (values - upper.astype(jnp.float32)).astype(jnp.bfloat16)
    total = jnp.dot(upper, sign_matrix, preferred_element_type=jnp.float32)
    total = total + jnp.dot(lower, sign_matrix, preferred_element_type=jnp.float32)
    return total * norm


def saturate(values):
    return jnp.clip(values, -saturation, saturation)


def fused_kernel(
    count,
    query_part,
    memory_part,
    out_weight_hbm,
    document_row,
    query_exponent,
    partial_exponent,
    summed_exponent,
    out_exponent,
    relevel,
    sign_ref,
    cosine_ref,
    sine_ref,
    out_ref,
    out_weight,
    first_near_send,
    first_near_recv,
    first_far_send,
    first_far_recv,
    memory_pair,
    mixed,
    second_near_send,
    second_near_recv,
    second_far_send,
    second_far_recv,
    first_total,
    total,
    bias,
    weight_sem,
    near_send_sem,
    near_recv_sem,
    far_send_sem,
    far_recv_sem,
    pair_send_sem,
    pair_recv_sem,
    piece_near_send,
    piece_near_recv,
    piece_far_send,
    piece_far_recv,
    out_send_sem,
    out_recv_sem,
):
    me = lax.axis_index("gx")
    core = lax.axis_index("gy")
    mate = 1 - core
    columns_of = count // 2
    column, row = me // 2, lax.rem(me, 2)
    neighbour = column * 2 + 1 - row
    length, width = query_part.shape[1], query_part.shape[2]
    span = out_ref.shape[2]
    blocks = span // width
    norm = 1.0 / math.sqrt(width)
    chunk = 2 * width
    mesh_ids = pl.DeviceIdType.MESH

    load = pltpu.make_async_copy(out_weight_hbm, out_weight, weight_sem)
    load.start()

    def column_at(step):
        return lax.rem(column + 1 + step, columns_of)

    barrier = pltpu.get_barrier_semaphore()
    pl.semaphore_signal(barrier, inc=1, device_id={"gy": mate}, device_id_type=mesh_ids)
    pl.semaphore_signal(barrier, inc=1, device_id={"gx": neighbour}, device_id_type=mesh_ids)
    for step in range(columns_of - 1):
        pl.semaphore_signal(
            barrier,
            inc=1,
            device_id={"gx": column_at(step) * 2 + row},
            device_id_type=mesh_ids,
        )
    pl.semaphore_wait(barrier, columns_of + 1)

    small_signs = sign_ref[:width, :width]

    def first_near_copy(kind, step):
        return pltpu.make_async_remote_copy(
            src_ref=first_near_send.at[kind, step],
            dst_ref=first_near_recv.at[kind, step],
            send_sem=near_send_sem.at[kind, step],
            recv_sem=near_recv_sem.at[kind, step],
            device_id={"gx": neighbour},
            device_id_type=mesh_ids,
        )

    def first_far_copy(kind, step):
        return pltpu.make_async_remote_copy(
            src_ref=first_far_send.at[kind, step],
            dst_ref=first_far_recv.at[kind, step],
            send_sem=far_send_sem.at[kind, step],
            recv_sem=far_recv_sem.at[kind, step],
            device_id={"gx": column_at(step) * 2 + row},
            device_id_type=mesh_ids,
        )

    def pair_copy(ref, place):
        return pltpu.make_async_remote_copy(
            src_ref=ref.at[core],
            dst_ref=ref.at[core],
            send_sem=pair_send_sem.at[place],
            recv_sem=pair_recv_sem.at[place],
            device_id={"gy": mate},
            device_id_type=mesh_ids,
        )

    def query_term(target):
        scale = power(-query_exponent[target, 0], width)
        return saturate(turn(query_part[target], small_signs, norm) * scale)

    def memory_term(target):
        scale = power(-partial_exponent[core, target], width)
        return saturate(turn(memory_part[core, target], small_signs, norm) * scale)

    terms = (memory_term, query_term)

    def first_near(step, carry):
        target = column_at(step) * 2 + 1 - row
        for kind, term in enumerate(terms):
            first_near_send[kind, step] = term(target).astype(jnp.bfloat16)
            first_near_copy(kind, step).start()
        return carry

    def first_joined(kind, step):
        term = terms[kind](column_at(step) * 2 + row)
        first_near_copy(kind, step).wait_recv()
        return term + first_near_recv[kind, step].astype(jnp.float32)

    def first_far(step, carry):
        first_near(step + 1, 0)
        for kind in range(2):
            first_far_send[kind, step] = first_joined(kind, step).astype(jnp.bfloat16)
            first_far_copy(kind, step).start()
        return carry

    first_near(0, 0)
    lax.fori_loop(0, columns_of - 1, first_far, 0)
    for kind in range(2):
        first_total[kind] = first_joined(kind, columns_of - 1)

    rows = lax.broadcasted_iota(jnp.int32, (length, length), 0)
    columns = lax.broadcasted_iota(jnp.int32, (length, length), 1)
    documents = jnp.broadcast_to(document_row[...], (length, length)).astype(jnp.float32)
    allowed = (rows >= columns) & (documents.T == documents)
    bias[...] = jnp.where(allowed, 0.0, -jnp.inf)

    def first_sum(kind, step):
        first_far_copy(kind, step).wait_recv()
        first_total[kind] += first_far_recv[kind, step].astype(jnp.float32)

    for step in range(columns_of - 1):
        first_sum(0, step)
        if step + 2 < columns_of:
            first_sum(1, step)

    level_ratio = power(partial_exponent[core, me] - summed_exponent[core, me], width)
    level = saturate(first_total[0] * level_ratio)
    memory = turn(level * power(summed_exponent[core, me], width), small_signs, norm)
    turned = memory * cosine_ref[...] + pltpu.roll(memory, width // 2, 1) * sine_ref[...]
    memory_pair[core] = jnp.where(core == 0, turned, memory).astype(jnp.bfloat16)
    pair_copy(memory_pair, 0).start()
    first_sum(1, columns_of - 2)
    query = turn(first_total[1] * power(query_exponent[me, 0], width), small_signs, norm)
    query = query * cosine_ref[...] + pltpu.roll(query, width // 2, 1) * sine_ref[...]
    query = query.astype(jnp.bfloat16)
    pair_copy(memory_pair, 0).wait_recv()

    scores = lax.dot_general(
        query, memory_pair[0], (((1,), (1,)), ((), ())), preferred_element_type=jnp.float32
    ) * (1.0 / math.sqrt(width))
    scores = scores + bias[...]
    exponentials = jnp.exp(scores - jnp.max(scores, axis=-1, keepdims=True))
    weights = exponentials / jnp.sum(exponentials, axis=-1, keepdims=True)
    mixed[core] = jnp.dot(
        weights.astype(jnp.bfloat16), memory_pair[1], preferred_element_type=jnp.float32
    ).astype(jnp.bfloat16)
    pair_copy(mixed, 1).start()
    load.wait()
    pair_copy(mixed, 1).wait_recv()

    def row_of(exponents):
        return jnp.concatenate([power(exponent, width) for exponent in exponents], axis=1)

    def second_term(target, part):
        start = pl.multiple_of((target * (span // chunk) + part) * chunk, chunk)
        both = jnp.concatenate([mixed[0], mixed[1]], axis=1)
        product = jnp.dot(
            both, out_weight[:, pl.ds(start, chunk)], preferred_element_type=jnp.float32
        )
        block = target * blocks + part * 2
        scale = row_of([-out_exponent[0, block], -out_exponent[0, block + 1]])
        return saturate(turn(product, sign_ref[...], norm) * scale)

    parts = span // chunk
    ahead = min(3, parts)
    near_total, far_total = columns_of * parts, (columns_of - 1) * parts

    def piece_copy(kind, piece):
        send, recv, send_sem, recv_sem, target = {
            "near": (second_near_send, second_near_recv, piece_near_send, piece_near_recv, None),
            "far": (second_far_send, second_far_recv, piece_far_send, piece_far_recv, 1),
        }[kind]
        if target is None:
            target = neighbour
        else:
            target = column_at(piece // parts) * 2 + row
        return pltpu.make_async_remote_copy(
            src_ref=send.at[piece],
            dst_ref=recv.at[piece],
            send_sem=send_sem.at[piece],
            recv_sem=recv_sem.at[piece],
            device_id={"gx": target},
            device_id_type=mesh_ids,
        )

    def second_near(piece, carry):
        target = column_at(piece // parts) * 2 + 1 - row
        second_near_send[piece] = second_term(target, piece % parts).astype(jnp.bfloat16)
        piece_copy("near", piece).start()
        return carry

    def second_joined(piece):
        term = second_term(column_at(piece // parts) * 2 + row, piece % parts)
        piece_copy("near", piece).wait_recv()
        return term + second_near_recv[piece].astype(jnp.float32)

    def second_far(piece, carry):
        second_near(piece + ahead, 0)
        second_far_send[piece] = second_joined(piece).astype(jnp.bfloat16)
        piece_copy("far", piece).start()
        return carry

    lax.fori_loop(0, ahead, second_near, 0)
    lax.fori_loop(0, far_total, second_far, 0)
    lax.fori_loop(far_total + ahead, near_total, second_near, 0)

    def second_own(part, carry):
        total[part] = second_joined(far_total + part)
        return carry

    lax.fori_loop(0, parts, second_own, 0)

    def second_sum(piece, carry):
        piece_copy("far", piece).wait_recv()
        total[piece % parts] += second_far_recv[piece].astype(jnp.float32)
        return carry

    lax.fori_loop(0, far_total - parts, second_sum, 0)

    def out_copy(part):
        place = slice(part * chunk, (part + 1) * chunk)
        return pltpu.make_async_remote_copy(
            src_ref=out_ref.at[core, :, place],
            dst_ref=out_ref.at[core, :, place],
            send_sem=out_send_sem.at[part],
            recv_sem=out_recv_sem.at[part],
            device_id={"gy": mate},
            device_id_type=mesh_ids,
        )

    for part in range(parts):
        second_sum(far_total - parts + part, 0)
        summed = [out_exponent[0, me * blocks + part * 2 + i] for i in range(2)]
        ending = [relevel[core, part * 2 + i] for i in range(2)]
        ratio = row_of([start - end for start, end in zip(summed, ending)])
        level = saturate(total[part] * ratio) * row_of(ending)
        out_ref[core, :, part * chunk : (part + 1) * chunk] = turn(
            level, sign_ref[...], norm
        ).astype(jnp.bfloat16)
        out_copy(part).start()

    def drain_near(step, carry):
        first_near_copy(0, step).wait_send()
        first_near_copy(1, step).wait_send()
        return carry

    def drain_far(step, carry):
        first_far_copy(0, step).wait_send()
        first_far_copy(1, step).wait_send()
        return carry

    def drain_near_piece(piece, carry):
        piece_copy("near", piece).wait_send()
        return carry

    def drain_far_piece(piece, carry):
        piece_copy("far", piece).wait_send()
        return carry

    lax.fori_loop(0, near_total, drain_near_piece, 0)
    lax.fori_loop(0, far_total, drain_far_piece, 0)
    lax.fori_loop(0, columns_of, drain_near, 0)
    lax.fori_loop(0, columns_of - 1, drain_far, 0)
    pair_copy(memory_pair, 0).wait_send()
    pair_copy(mixed, 1).wait_send()
    for part in range(parts):
        out_copy(part).wait()


def body(
    tokens,
    query_weight,
    key_value_projection_weight,
    output_weight,
    document_ids,
    query_exponent,
    key_value_partial_exponents,
    key_value_summed_exponents,
    output_exponent,
    output_relevel,
):
    count = lax.axis_size("gx")
    length = tokens.shape[0]
    width = query_weight.shape[3]
    heads = query_weight.shape[1]
    memory_heads = key_value_projection_weight.shape[2]
    span = output_weight.shape[1] // count
    even = count % 2 == 0 and lax.axis_size("gy") == 2 and span % (2 * width) == 0
    if not (even and count == heads == memory_heads):
        return plain_body(
            tokens,
            query_weight,
            key_value_projection_weight,
            output_weight,
            document_ids,
            query_exponent,
            key_value_partial_exponents,
            key_value_summed_exponents,
            output_exponent,
            output_relevel,
        )
    query_part = jnp.einsum(
        "sd,dpe->pse", tokens, query_weight[:, :, 0, :], preferred_element_type=jnp.float32
    )
    memory_part = jnp.einsum(
        "sd,dcne->cnse", tokens, key_value_projection_weight, preferred_element_type=jnp.float32
    )
    cosine, sine = rotary_tables(length, width)
    vmem = pl.BlockSpec(memory_space=pltpu.VMEM)
    smem = pl.BlockSpec(memory_space=pltpu.SMEM)
    half = count // 2
    parts = span // (2 * width)
    bf16 = jnp.bfloat16
    halves = pl.pallas_call(
        functools.partial(fused_kernel, count),
        out_shape=jax.ShapeDtypeStruct((2, length, span), bf16),
        in_specs=[vmem, vmem, pl.BlockSpec(memory_space=pl.ANY), vmem] + [smem] * 5 + [vmem] * 3,
        out_specs=vmem,
        scratch_shapes=[
            pltpu.VMEM(output_weight.shape, bf16),
            pltpu.VMEM((2, half, length, width), bf16),
            pltpu.VMEM((2, half, length, width), bf16),
            pltpu.VMEM((2, half - 1, length, width), bf16),
            pltpu.VMEM((2, half - 1, length, width), bf16),
            pltpu.VMEM((2, length, width), bf16),
            pltpu.VMEM((2, length, width), bf16),
            pltpu.VMEM((half * parts, length, 2 * width), bf16),
            pltpu.VMEM((half * parts, length, 2 * width), bf16),
            pltpu.VMEM(((half - 1) * parts, length, 2 * width), bf16),
            pltpu.VMEM(((half - 1) * parts, length, 2 * width), bf16),
            pltpu.VMEM((2, length, width), jnp.float32),
            pltpu.VMEM((parts, length, 2 * width), jnp.float32),
            pltpu.VMEM((length, length), jnp.float32),
            pltpu.SemaphoreType.DMA,
            pltpu.SemaphoreType.DMA((2, half)),
            pltpu.SemaphoreType.DMA((2, half)),
            pltpu.SemaphoreType.DMA((2, half - 1)),
            pltpu.SemaphoreType.DMA((2, half - 1)),
            pltpu.SemaphoreType.DMA((2,)),
            pltpu.SemaphoreType.DMA((2,)),
            pltpu.SemaphoreType.DMA((half * parts,)),
            pltpu.SemaphoreType.DMA((half * parts,)),
            pltpu.SemaphoreType.DMA(((half - 1) * parts,)),
            pltpu.SemaphoreType.DMA(((half - 1) * parts,)),
            pltpu.SemaphoreType.DMA((parts,)),
            pltpu.SemaphoreType.DMA((parts,)),
        ],
        compiler_params=pltpu.CompilerParams(
            collective_id=0, has_side_effects=True, vmem_limit_bytes=40 * 1024 * 1024
        ),
    )(
        query_part,
        memory_part,
        output_weight,
        document_ids[None, :],
        query_exponent,
        key_value_partial_exponents,
        key_value_summed_exponents,
        output_exponent,
        output_relevel,
        jnp.asarray(paired_signs(width), bf16),
        jnp.asarray(cosine),
        jnp.asarray(sine),
    )
    return halves.transpose(1, 0, 2)


def solution(mesh):
    return jax.shard_map(
        body,
        mesh=mesh,
        in_specs=(
            P("groups", "gx"),
            P("gx", None, "gy", None),
            P("gx", None, None, None),
            P("gx", "gy"),
            P("groups"),
            P(None, "gy"),
            P(),
            P(),
            P("gy", None),
            P(None, "gx"),
        ),
        out_specs=P("groups", None, "gx"),
        check_vma=False,
    )
```

```python
import functools
import math

import jax
import jax.numpy as jnp
import numpy as np
from jax import lax
from jax.experimental import pallas as pl
from jax.experimental.pallas import tpu as pltpu
from jax.sharding import PartitionSpec as P

rotary_base = 500000.0
saturation = 127.0


def hadamard(order):
    row_index = jnp.arange(order, dtype=jnp.int32)[:, None]
    col_index = jnp.arange(order, dtype=jnp.int32)[None, :]
    common = row_index & col_index
    parity = jnp.zeros((order, order), jnp.int32)
    for bit_place in range(order.bit_length() - 1):
        parity = parity ^ common >> bit_place & 1
    return (1 - 2 * parity).astype(jnp.float32) * (1.0 / math.sqrt(order))


def rotate(values, rotation):
    return jnp.matmul(values, rotation, precision=lax.Precision.HIGHEST)


def rotary(values):
    length = values.shape[-2]
    full_width = values.shape[-1]
    half_width = full_width // 2
    frequency = rotary_base ** (-(jnp.arange(half_width, dtype=jnp.float32) * 2.0 / full_width))
    places = jnp.arange(length, dtype=jnp.int32).astype(jnp.float32)
    angles = places[:, None] * frequency[None, :]
    cosine = jnp.cos(angles)
    sine_part = jnp.sin(angles)
    front_half = values[..., :half_width]
    back_half = values[..., half_width:]
    return jnp.concatenate(
        [front_half * cosine - back_half * sine_part, back_half * cosine + front_half * sine_part],
        axis=-1,
    )


def plain_body(
    tokens,
    query_weight,
    key_value_projection_weight,
    output_weight,
    document_ids,
    query_exponent,
    key_value_partial_exponents,
    key_value_summed_exponents,
    output_exponent,
    output_relevel,
):
    length = tokens.shape[0]
    head_width = query_weight.shape[3]
    memory_heads = key_value_projection_weight.shape[2]
    count_gx = lax.axis_size("gx")
    where_gx = lax.axis_index("gx")
    where_gy = lax.axis_index("gy")
    rotation = hadamard(head_width)
    query_block = query_weight[:, :, 0, :]
    query_inverse = jnp.exp2(-query_exponent[:, 0].astype(jnp.float32))
    query_up = jnp.exp2(query_exponent[:, 0].astype(jnp.float32))
    heads_total = query_block.shape[1]
    heads_here = heads_total // count_gx
    heads_spread = count_gx // memory_heads
    memory_index = where_gx // heads_spread
    memory_inverse = jnp.exp2(-key_value_partial_exponents.astype(jnp.float32))
    memory_up = jnp.exp2(key_value_partial_exponents.astype(jnp.float32))
    memory_scale = jnp.exp2(key_value_summed_exponents.astype(jnp.float32))
    partial_sum = jnp.einsum("sd,dpe->pse", tokens, query_block, preferred_element_type=jnp.float32)
    factor = query_inverse
    query_sum = lax.psum_scatter(
        jnp.clip(rotate(partial_sum, rotation) * factor[:, None, None], -saturation, saturation),
        "gx",
        scatter_dimension=0,
        tiled=True,
    )
    query_scale = lax.dynamic_slice_in_dim(query_up, where_gx * heads_here, heads_here, 0)
    query = rotary(rotate(query_sum * query_scale[:, None, None], rotation))[0].astype(jnp.bfloat16)
    partial_sum = jnp.einsum(
        "sd,dche->sche", tokens, key_value_projection_weight, preferred_element_type=jnp.float32
    )
    memory_sum = lax.psum_scatter(
        jnp.clip(
            rotate(partial_sum, rotation) * memory_inverse[None, :, :, None],
            -saturation,
            saturation,
        ),
        "gx",
        scatter_dimension=0,
        tiled=True,
    )
    whole = lax.all_gather(
        jnp.clip(
            memory_sum * memory_up[None, :, :, None] / memory_scale[None, :, :, None],
            -saturation,
            saturation,
        ),
        "gx",
        axis=0,
        tiled=True,
    )
    arrived = lax.dynamic_index_in_dim(whole, memory_index, 2, keepdims=False)
    head_scale = lax.dynamic_index_in_dim(memory_scale, memory_index, 1, keepdims=False)
    memory_full = rotate(arrived * head_scale[None, :, None], rotation)
    keys = rotary(memory_full[:, 0]).astype(jnp.bfloat16)
    values = memory_full[:, 1].astype(jnp.bfloat16)
    scores = jnp.einsum("qe,ke->qk", query, keys, preferred_element_type=jnp.float32) * (
        1.0 / math.sqrt(head_width)
    )
    position = jnp.arange(length, dtype=jnp.int32)
    allowed = (position[:, None] >= position[None, :]) & (
        document_ids[:, None] == document_ids[None, :]
    )
    scores = jnp.where(allowed, scores, -jnp.inf)
    row_max = jnp.max(scores, axis=-1, keepdims=True)
    exponentials = jnp.exp(scores - row_max)
    weights = (exponentials / jnp.sum(exponentials, axis=-1, keepdims=True)).astype(jnp.bfloat16)
    attended = jnp.dot(weights, values, preferred_element_type=jnp.float32).astype(jnp.bfloat16)
    head_pairs = lax.all_gather(attended, "gy", axis=1, tiled=True)
    feature_blocks = output_weight.shape[1] // head_width
    blocks_here = feature_blocks // count_gx
    output_inverse = jnp.exp2(-output_exponent[0].astype(jnp.float32))
    partial_sum = jnp.dot(head_pairs, output_weight, preferred_element_type=jnp.float32)
    partial_sum = partial_sum.reshape(
        length, blocks_here * lax.axis_size("gx"), head_width
    ).transpose(1, 0, 2)
    factor = output_inverse
    out_sum = lax.psum_scatter(
        jnp.clip(rotate(partial_sum, rotation) * factor[:, None, None], -saturation, saturation),
        "gx",
        scatter_dimension=0,
        tiled=True,
    )
    out_up = jnp.exp2(
        lax.dynamic_slice_in_dim(output_exponent[0], where_gx * blocks_here, blocks_here, 0).astype(
            jnp.float32
        )
    )
    own_scale = jnp.exp2(
        lax.dynamic_index_in_dim(output_relevel, where_gy, 0, keepdims=False).astype(jnp.float32)
    )
    out_level = jnp.clip(
        out_sum * out_up[:, None, None] / own_scale[:, None, None], -saturation, saturation
    )
    halves = lax.all_gather(out_level[None], "gy", axis=0, tiled=True)
    restored = rotate(
        halves * jnp.exp2(output_relevel.astype(jnp.float32))[:, :, None, None], rotation
    )
    return (
        restored.transpose(2, 0, 1, 3)
        .reshape(length, 2, blocks_here * head_width)
        .astype(jnp.bfloat16)
    )


def signs(order):
    index = np.arange(order)
    common = index[:, None] & index[None, :]
    parity = np.zeros((order, order), np.int64)
    for place in range(order.bit_length() - 1):
        parity ^= (common >> place) & 1
    return 1.0 - 2.0 * parity


def paired_signs(order):
    return np.kron(np.eye(2), signs(order))


def rotary_tables(length, width):
    half = width // 2
    frequency = rotary_base ** (-(np.arange(half, dtype=np.float64) * 2.0 / width))
    angles = np.arange(length)[:, None] * frequency.astype(np.float32).astype(np.float64)[None, :]
    cosine = np.concatenate([np.cos(angles), np.cos(angles)], axis=1)
    sine = np.concatenate([-np.sin(angles), np.sin(angles)], axis=1)
    return cosine.astype(np.float32), sine.astype(np.float32)


def power(exponent, width):
    row = jnp.full((1, width), exponent, jnp.int32)
    size = jnp.abs(row)
    upward = jnp.ones((1, width), jnp.float32)
    downward = jnp.ones((1, width), jnp.float32)
    for place in (1, 2, 4, 8, 16):
        taken = (size & place) != 0
        upward = jnp.where(taken, upward * 2.0**place, upward)
        downward = jnp.where(taken, downward * 2.0**-place, downward)
    return jnp.where(row >= 0, upward, downward)


def turn(values, sign_matrix, norm):
    upper = values.astype(jnp.bfloat16)
    lower = (values - upper.astype(jnp.float32)).astype(jnp.bfloat16)
    total = jnp.dot(upper, sign_matrix, preferred_element_type=jnp.float32)
    total = total + jnp.dot(lower, sign_matrix, preferred_element_type=jnp.float32)
    return total * norm


def saturate(values):
    return jnp.clip(values, -saturation, saturation)


def fused_kernel(
    count,
    query_part,
    memory_part,
    out_weight_hbm,
    document_row,
    query_exponent,
    partial_exponent,
    summed_exponent,
    out_exponent,
    relevel,
    sign_ref,
    cosine_ref,
    sine_ref,
    out_ref,
    out_weight,
    first_near_send,
    first_near_recv,
    first_far_send,
    first_far_recv,
    memory_pair,
    mixed,
    second_near_send,
    second_near_recv,
    second_far_send,
    second_far_recv,
    first_total,
    total,
    bias,
    weight_sem,
    near_send_sem,
    near_recv_sem,
    far_send_sem,
    far_recv_sem,
    pair_send_sem,
    pair_recv_sem,
    piece_near_send,
    piece_near_recv,
    piece_far_send,
    piece_far_recv,
    out_send_sem,
    out_recv_sem,
):
    me = lax.axis_index("gx")
    core = lax.axis_index("gy")
    mate = 1 - core
    columns_of = count // 2
    column, row = me // 2, lax.rem(me, 2)
    neighbour = column * 2 + 1 - row
    length, width = query_part.shape[1], query_part.shape[2]
    span = out_ref.shape[2]
    blocks = span // width
    norm = 1.0 / math.sqrt(width)
    chunk = 2 * width
    mesh_ids = pl.DeviceIdType.MESH

    load = pltpu.make_async_copy(out_weight_hbm, out_weight, weight_sem)
    load.start()

    def column_at(step):
        return lax.rem(column + 1 + step, columns_of)

    barrier = pltpu.get_barrier_semaphore()
    pl.semaphore_signal(barrier, inc=1, device_id={"gy": mate}, device_id_type=mesh_ids)
    pl.semaphore_signal(barrier, inc=1, device_id={"gx": neighbour}, device_id_type=mesh_ids)
    for step in range(columns_of - 1):
        pl.semaphore_signal(
            barrier,
            inc=1,
            device_id={"gx": column_at(step) * 2 + row},
            device_id_type=mesh_ids,
        )
    pl.semaphore_wait(barrier, columns_of + 1)

    small_signs = sign_ref[:width, :width]

    def first_near_copy(kind, step):
        return pltpu.make_async_remote_copy(
            src_ref=first_near_send.at[kind, step],
            dst_ref=first_near_recv.at[kind, step],
            send_sem=near_send_sem.at[kind, step],
            recv_sem=near_recv_sem.at[kind, step],
            device_id={"gx": neighbour},
            device_id_type=mesh_ids,
        )

    def first_far_copy(kind, step):
        return pltpu.make_async_remote_copy(
            src_ref=first_far_send.at[kind, step],
            dst_ref=first_far_recv.at[kind, step],
            send_sem=far_send_sem.at[kind, step],
            recv_sem=far_recv_sem.at[kind, step],
            device_id={"gx": column_at(step) * 2 + row},
            device_id_type=mesh_ids,
        )

    def pair_copy(ref, place):
        return pltpu.make_async_remote_copy(
            src_ref=ref.at[core],
            dst_ref=ref.at[core],
            send_sem=pair_send_sem.at[place],
            recv_sem=pair_recv_sem.at[place],
            device_id={"gy": mate},
            device_id_type=mesh_ids,
        )

    def query_term(target):
        scale = power(-query_exponent[0, target], width)
        return saturate(turn(query_part[target], small_signs, norm) * scale)

    def memory_term(target):
        scale = power(-partial_exponent[core, target], width)
        return saturate(turn(memory_part[core, target], small_signs, norm) * scale)

    terms = (memory_term, query_term)

    def first_near(step, carry):
        target = column_at(step) * 2 + 1 - row
        for kind, term in enumerate(terms):
            first_near_send[kind, step] = term(target).astype(jnp.bfloat16)
            first_near_copy(kind, step).start()
        return carry

    def first_joined(kind, step):
        term = terms[kind](column_at(step) * 2 + row)
        first_near_copy(kind, step).wait_recv()
        return term + first_near_recv[kind, step].astype(jnp.float32)

    def first_far(step, carry):
        first_near(step + 1, 0)
        for kind in range(2):
            first_far_send[kind, step] = first_joined(kind, step).astype(jnp.bfloat16)
            first_far_copy(kind, step).start()
        return carry

    first_near(0, 0)
    lax.fori_loop(0, columns_of - 1, first_far, 0)
    for kind in range(2):
        first_total[kind] = first_joined(kind, columns_of - 1)

    rows = lax.broadcasted_iota(jnp.int32, (length, length), 0)
    columns = lax.broadcasted_iota(jnp.int32, (length, length), 1)
    documents = jnp.broadcast_to(document_row[...], (length, length)).astype(jnp.float32)
    allowed = (rows >= columns) & (documents.T == documents)
    bias[...] = jnp.where(allowed, 0.0, -jnp.inf)

    def first_sum(kind, step):
        first_far_copy(kind, step).wait_recv()
        first_total[kind] += first_far_recv[kind, step].astype(jnp.float32)

    for step in range(columns_of - 1):
        first_sum(0, step)
        if step + 2 < columns_of:
            first_sum(1, step)

    level_ratio = power(partial_exponent[core, me] - summed_exponent[core, me], width)
    level = saturate(first_total[0] * level_ratio)
    memory = turn(level * power(summed_exponent[core, me], width), small_signs, norm)
    turned = memory * cosine_ref[...] + pltpu.roll(memory, width // 2, 1) * sine_ref[...]
    memory_pair[core] = jnp.where(core == 0, turned, memory).astype(jnp.bfloat16)
    pair_copy(memory_pair, 0).start()
    first_sum(1, columns_of - 2)
    query = turn(first_total[1] * power(query_exponent[0, me], width), small_signs, norm)
    query = query * cosine_ref[...] + pltpu.roll(query, width // 2, 1) * sine_ref[...]
    query = query.astype(jnp.bfloat16)
    pair_copy(memory_pair, 0).wait_recv()

    scores = lax.dot_general(
        query, memory_pair[0], (((1,), (1,)), ((), ())), preferred_element_type=jnp.float32
    ) * (1.0 / math.sqrt(width))
    scores = scores + bias[...]
    exponentials = jnp.exp(scores - jnp.max(scores, axis=-1, keepdims=True))
    weights = exponentials / jnp.sum(exponentials, axis=-1, keepdims=True)
    mixed[core] = jnp.dot(
        weights.astype(jnp.bfloat16), memory_pair[1], preferred_element_type=jnp.float32
    ).astype(jnp.bfloat16)
    pair_copy(mixed, 1).start()
    load.wait()
    pair_copy(mixed, 1).wait_recv()

    def row_of(exponents):
        return jnp.concatenate([power(exponent, width) for exponent in exponents], axis=1)

    def second_term(target, part):
        start = pl.multiple_of((target * (span // chunk) + part) * chunk, chunk)
        both = jnp.concatenate([mixed[0], mixed[1]], axis=1)
        product = jnp.dot(
            both, out_weight[:, pl.ds(start, chunk)], preferred_element_type=jnp.float32
        )
        block = target * blocks + part * 2
        scale = row_of([-out_exponent[0, block], -out_exponent[0, block + 1]])
        return saturate(turn(product, sign_ref[...], norm) * scale)

    parts = span // chunk
    ahead = parts
    near_total, far_total = columns_of * parts, (columns_of - 1) * parts

    def piece_copy(kind, piece):
        send, recv, send_sem, recv_sem, target = {
            "near": (second_near_send, second_near_recv, piece_near_send, piece_near_recv, None),
            "far": (second_far_send, second_far_recv, piece_far_send, piece_far_recv, 1),
        }[kind]
        if target is None:
            target = neighbour
        else:
            target = column_at(piece // parts) * 2 + row
        return pltpu.make_async_remote_copy(
            src_ref=send.at[piece],
            dst_ref=recv.at[piece],
            send_sem=send_sem.at[piece],
            recv_sem=recv_sem.at[piece],
            device_id={"gx": target},
            device_id_type=mesh_ids,
        )

    def second_near(piece, carry):
        target = column_at(piece // parts) * 2 + 1 - row
        second_near_send[piece] = second_term(target, piece % parts).astype(jnp.bfloat16)
        piece_copy("near", piece).start()
        return carry

    def second_joined(piece):
        term = second_term(column_at(piece // parts) * 2 + row, piece % parts)
        piece_copy("near", piece).wait_recv()
        return term + second_near_recv[piece].astype(jnp.float32)

    def second_far(piece, carry):
        second_near(piece + ahead, 0)
        second_far_send[piece] = second_joined(piece).astype(jnp.bfloat16)
        piece_copy("far", piece).start()
        return carry

    lax.fori_loop(0, ahead, second_near, 0)
    lax.fori_loop(0, far_total, second_far, 0)
    lax.fori_loop(far_total + ahead, near_total, second_near, 0)

    def second_own(part, carry):
        total[part] = second_joined(far_total + part)
        return carry

    lax.fori_loop(0, parts, second_own, 0)

    def second_sum(piece, carry):
        piece_copy("far", piece).wait_recv()
        total[piece % parts] += second_far_recv[piece].astype(jnp.float32)
        return carry

    lax.fori_loop(0, far_total - parts, second_sum, 0)

    def out_copy(part):
        place = slice(part * chunk, (part + 1) * chunk)
        return pltpu.make_async_remote_copy(
            src_ref=out_ref.at[core, :, place],
            dst_ref=out_ref.at[core, :, place],
            send_sem=out_send_sem.at[part],
            recv_sem=out_recv_sem.at[part],
            device_id={"gy": mate},
            device_id_type=mesh_ids,
        )

    for part in range(parts):
        second_sum(far_total - parts + part, 0)
        summed = [out_exponent[0, me * blocks + part * 2 + i] for i in range(2)]
        ending = [relevel[core, part * 2 + i] for i in range(2)]
        ratio = row_of([start - end for start, end in zip(summed, ending)])
        level = saturate(total[part] * ratio) * row_of(ending)
        out_ref[core, :, part * chunk : (part + 1) * chunk] = turn(
            level, sign_ref[...], norm
        ).astype(jnp.bfloat16)
        out_copy(part).start()

    def drain_near(step, carry):
        first_near_copy(0, step).wait_send()
        first_near_copy(1, step).wait_send()
        return carry

    def drain_far(step, carry):
        first_far_copy(0, step).wait_send()
        first_far_copy(1, step).wait_send()
        return carry

    def drain_near_piece(piece, carry):
        piece_copy("near", piece).wait_send()
        return carry

    def drain_far_piece(piece, carry):
        piece_copy("far", piece).wait_send()
        return carry

    lax.fori_loop(0, near_total, drain_near_piece, 0)
    lax.fori_loop(0, far_total, drain_far_piece, 0)
    lax.fori_loop(0, columns_of, drain_near, 0)
    lax.fori_loop(0, columns_of - 1, drain_far, 0)
    pair_copy(memory_pair, 0).wait_send()
    pair_copy(mixed, 1).wait_send()
    for part in range(parts):
        out_copy(part).wait()


def body(
    tokens,
    query_weight,
    key_value_projection_weight,
    output_weight,
    document_ids,
    query_exponent,
    key_value_partial_exponents,
    key_value_summed_exponents,
    output_exponent,
    output_relevel,
):
    count = lax.axis_size("gx")
    length = tokens.shape[0]
    width = query_weight.shape[3]
    heads = query_weight.shape[1]
    memory_heads = key_value_projection_weight.shape[2]
    span = output_weight.shape[1] // count
    even = count % 2 == 0 and lax.axis_size("gy") == 2 and span % (2 * width) == 0
    if not (even and count == heads == memory_heads):
        return plain_body(
            tokens,
            query_weight,
            key_value_projection_weight,
            output_weight,
            document_ids,
            query_exponent,
            key_value_partial_exponents,
            key_value_summed_exponents,
            output_exponent,
            output_relevel,
        )
    query_part = jnp.einsum(
        "sd,dpe->pse", tokens, query_weight[:, :, 0, :], preferred_element_type=jnp.float32
    )
    memory_part = jnp.einsum(
        "sd,dcne->cnse", tokens, key_value_projection_weight, preferred_element_type=jnp.float32
    )
    cosine, sine = rotary_tables(length, width)
    vmem = pl.BlockSpec(memory_space=pltpu.VMEM)
    smem = pl.BlockSpec(memory_space=pltpu.SMEM)
    half = count // 2
    parts = span // (2 * width)
    bf16 = jnp.bfloat16
    halves = pl.pallas_call(
        functools.partial(fused_kernel, count),
        out_shape=jax.ShapeDtypeStruct((2, length, span), bf16),
        in_specs=[vmem, vmem, pl.BlockSpec(memory_space=pl.ANY), vmem] + [smem] * 5 + [vmem] * 3,
        out_specs=vmem,
        scratch_shapes=[
            pltpu.VMEM(output_weight.shape, bf16),
            pltpu.VMEM((2, half, length, width), bf16),
            pltpu.VMEM((2, half, length, width), bf16),
            pltpu.VMEM((2, half - 1, length, width), bf16),
            pltpu.VMEM((2, half - 1, length, width), bf16),
            pltpu.VMEM((2, length, width), bf16),
            pltpu.VMEM((2, length, width), bf16),
            pltpu.VMEM((half * parts, length, 2 * width), bf16),
            pltpu.VMEM((half * parts, length, 2 * width), bf16),
            pltpu.VMEM(((half - 1) * parts, length, 2 * width), bf16),
            pltpu.VMEM(((half - 1) * parts, length, 2 * width), bf16),
            pltpu.VMEM((2, length, width), jnp.float32),
            pltpu.VMEM((parts, length, 2 * width), jnp.float32),
            pltpu.VMEM((length, length), jnp.float32),
            pltpu.SemaphoreType.DMA,
            pltpu.SemaphoreType.DMA((2, half)),
            pltpu.SemaphoreType.DMA((2, half)),
            pltpu.SemaphoreType.DMA((2, half - 1)),
            pltpu.SemaphoreType.DMA((2, half - 1)),
            pltpu.SemaphoreType.DMA((2,)),
            pltpu.SemaphoreType.DMA((2,)),
            pltpu.SemaphoreType.DMA((half * parts,)),
            pltpu.SemaphoreType.DMA((half * parts,)),
            pltpu.SemaphoreType.DMA(((half - 1) * parts,)),
            pltpu.SemaphoreType.DMA(((half - 1) * parts,)),
            pltpu.SemaphoreType.DMA((parts,)),
            pltpu.SemaphoreType.DMA((parts,)),
        ],
        compiler_params=pltpu.CompilerParams(
            collective_id=0, has_side_effects=True, vmem_limit_bytes=40 * 1024 * 1024
        ),
    )(
        query_part,
        memory_part,
        output_weight,
        document_ids[None, :],
        query_exponent.T,
        key_value_partial_exponents,
        key_value_summed_exponents,
        output_exponent,
        output_relevel,
        jnp.asarray(paired_signs(width), bf16),
        jnp.asarray(cosine),
        jnp.asarray(sine),
    )
    return halves.transpose(1, 0, 2)


def solution(mesh):
    return jax.shard_map(
        body,
        mesh=mesh,
        in_specs=(
            P("groups", "gx"),
            P("gx", None, "gy", None),
            P("gx", None, None, None),
            P("gx", "gy"),
            P("groups"),
            P(None, "gy"),
            P(),
            P(),
            P("gy", None),
            P(None, "gx"),
        ),
        out_specs=P("groups", None, "gx"),
        check_vma=False,
    )
```

```python
import functools
import math

import jax
import jax.numpy as jnp
import numpy as np
from jax import lax
from jax.experimental import pallas as pl
from jax.experimental.pallas import tpu as pltpu
from jax.sharding import PartitionSpec as P

rotary_base = 500000.0
saturation = 127.0


def hadamard(order):
    row_index = jnp.arange(order, dtype=jnp.int32)[:, None]
    col_index = jnp.arange(order, dtype=jnp.int32)[None, :]
    common = row_index & col_index
    parity = jnp.zeros((order, order), jnp.int32)
    for bit_place in range(order.bit_length() - 1):
        parity = parity ^ common >> bit_place & 1
    return (1 - 2 * parity).astype(jnp.float32) * (1.0 / math.sqrt(order))


def rotate(values, rotation):
    return jnp.matmul(values, rotation, precision=lax.Precision.HIGHEST)


def rotary(values):
    length = values.shape[-2]
    full_width = values.shape[-1]
    half_width = full_width // 2
    frequency = rotary_base ** (-(jnp.arange(half_width, dtype=jnp.float32) * 2.0 / full_width))
    places = jnp.arange(length, dtype=jnp.int32).astype(jnp.float32)
    angles = places[:, None] * frequency[None, :]
    cosine = jnp.cos(angles)
    sine_part = jnp.sin(angles)
    front_half = values[..., :half_width]
    back_half = values[..., half_width:]
    return jnp.concatenate(
        [front_half * cosine - back_half * sine_part, back_half * cosine + front_half * sine_part],
        axis=-1,
    )


def plain_body(
    tokens,
    query_weight,
    key_value_projection_weight,
    output_weight,
    document_ids,
    query_exponent,
    key_value_partial_exponents,
    key_value_summed_exponents,
    output_exponent,
    output_relevel,
):
    length = tokens.shape[0]
    head_width = query_weight.shape[3]
    memory_heads = key_value_projection_weight.shape[2]
    count_gx = lax.axis_size("gx")
    where_gx = lax.axis_index("gx")
    where_gy = lax.axis_index("gy")
    rotation = hadamard(head_width)
    query_block = query_weight[:, :, 0, :]
    query_inverse = jnp.exp2(-query_exponent[:, 0].astype(jnp.float32))
    query_up = jnp.exp2(query_exponent[:, 0].astype(jnp.float32))
    heads_total = query_block.shape[1]
    heads_here = heads_total // count_gx
    heads_spread = count_gx // memory_heads
    memory_index = where_gx // heads_spread
    memory_inverse = jnp.exp2(-key_value_partial_exponents.astype(jnp.float32))
    memory_up = jnp.exp2(key_value_partial_exponents.astype(jnp.float32))
    memory_scale = jnp.exp2(key_value_summed_exponents.astype(jnp.float32))
    partial_sum = jnp.einsum("sd,dpe->pse", tokens, query_block, preferred_element_type=jnp.float32)
    factor = query_inverse
    query_sum = lax.psum_scatter(
        jnp.clip(rotate(partial_sum, rotation) * factor[:, None, None], -saturation, saturation),
        "gx",
        scatter_dimension=0,
        tiled=True,
    )
    query_scale = lax.dynamic_slice_in_dim(query_up, where_gx * heads_here, heads_here, 0)
    query = rotary(rotate(query_sum * query_scale[:, None, None], rotation))[0].astype(jnp.bfloat16)
    partial_sum = jnp.einsum(
        "sd,dche->sche", tokens, key_value_projection_weight, preferred_element_type=jnp.float32
    )
    memory_sum = lax.psum_scatter(
        jnp.clip(
            rotate(partial_sum, rotation) * memory_inverse[None, :, :, None],
            -saturation,
            saturation,
        ),
        "gx",
        scatter_dimension=0,
        tiled=True,
    )
    whole = lax.all_gather(
        jnp.clip(
            memory_sum * memory_up[None, :, :, None] / memory_scale[None, :, :, None],
            -saturation,
            saturation,
        ),
        "gx",
        axis=0,
        tiled=True,
    )
    arrived = lax.dynamic_index_in_dim(whole, memory_index, 2, keepdims=False)
    head_scale = lax.dynamic_index_in_dim(memory_scale, memory_index, 1, keepdims=False)
    memory_full = rotate(arrived * head_scale[None, :, None], rotation)
    keys = rotary(memory_full[:, 0]).astype(jnp.bfloat16)
    values = memory_full[:, 1].astype(jnp.bfloat16)
    scores = jnp.einsum("qe,ke->qk", query, keys, preferred_element_type=jnp.float32) * (
        1.0 / math.sqrt(head_width)
    )
    position = jnp.arange(length, dtype=jnp.int32)
    allowed = (position[:, None] >= position[None, :]) & (
        document_ids[:, None] == document_ids[None, :]
    )
    scores = jnp.where(allowed, scores, -jnp.inf)
    row_max = jnp.max(scores, axis=-1, keepdims=True)
    exponentials = jnp.exp(scores - row_max)
    weights = (exponentials / jnp.sum(exponentials, axis=-1, keepdims=True)).astype(jnp.bfloat16)
    attended = jnp.dot(weights, values, preferred_element_type=jnp.float32).astype(jnp.bfloat16)
    head_pairs = lax.all_gather(attended, "gy", axis=1, tiled=True)
    feature_blocks = output_weight.shape[1] // head_width
    blocks_here = feature_blocks // count_gx
    output_inverse = jnp.exp2(-output_exponent[0].astype(jnp.float32))
    partial_sum = jnp.dot(head_pairs, output_weight, preferred_element_type=jnp.float32)
    partial_sum = partial_sum.reshape(
        length, blocks_here * lax.axis_size("gx"), head_width
    ).transpose(1, 0, 2)
    factor = output_inverse
    out_sum = lax.psum_scatter(
        jnp.clip(rotate(partial_sum, rotation) * factor[:, None, None], -saturation, saturation),
        "gx",
        scatter_dimension=0,
        tiled=True,
    )
    out_up = jnp.exp2(
        lax.dynamic_slice_in_dim(output_exponent[0], where_gx * blocks_here, blocks_here, 0).astype(
            jnp.float32
        )
    )
    own_scale = jnp.exp2(
        lax.dynamic_index_in_dim(output_relevel, where_gy, 0, keepdims=False).astype(jnp.float32)
    )
    out_level = jnp.clip(
        out_sum * out_up[:, None, None] / own_scale[:, None, None], -saturation, saturation
    )
    halves = lax.all_gather(out_level[None], "gy", axis=0, tiled=True)
    restored = rotate(
        halves * jnp.exp2(output_relevel.astype(jnp.float32))[:, :, None, None], rotation
    )
    return (
        restored.transpose(2, 0, 1, 3)
        .reshape(length, 2, blocks_here * head_width)
        .astype(jnp.bfloat16)
    )


def signs(order):
    index = np.arange(order)
    common = index[:, None] & index[None, :]
    parity = np.zeros((order, order), np.int64)
    for place in range(order.bit_length() - 1):
        parity ^= (common >> place) & 1
    return 1.0 - 2.0 * parity


def paired_signs(order):
    return np.kron(np.eye(2), signs(order))


def rotary_tables(length, width):
    half = width // 2
    frequency = rotary_base ** (-(np.arange(half, dtype=np.float64) * 2.0 / width))
    angles = np.arange(length)[:, None] * frequency.astype(np.float32).astype(np.float64)[None, :]
    cosine = np.concatenate([np.cos(angles), np.cos(angles)], axis=1)
    sine = np.concatenate([-np.sin(angles), np.sin(angles)], axis=1)
    return cosine.astype(np.float32), sine.astype(np.float32)


def power(exponent, width):
    row = jnp.full((1, width), exponent, jnp.int32)
    size = jnp.abs(row)
    upward = jnp.ones((1, width), jnp.float32)
    downward = jnp.ones((1, width), jnp.float32)
    for place in (1, 2, 4, 8, 16):
        taken = (size & place) != 0
        upward = jnp.where(taken, upward * 2.0**place, upward)
        downward = jnp.where(taken, downward * 2.0**-place, downward)
    return jnp.where(row >= 0, upward, downward)


def turn(values, sign_matrix, norm):
    upper = values.astype(jnp.bfloat16)
    lower = (values - upper.astype(jnp.float32)).astype(jnp.bfloat16)
    total = jnp.dot(upper, sign_matrix, preferred_element_type=jnp.float32)
    total = total + jnp.dot(lower, sign_matrix, preferred_element_type=jnp.float32)
    return total * norm


def saturate(values):
    return jnp.clip(values, -saturation, saturation)


def fused_kernel(
    count,
    query_part,
    memory_part,
    out_weight_hbm,
    document_row,
    query_exponent,
    partial_exponent,
    summed_exponent,
    out_exponent,
    relevel,
    sign_ref,
    cosine_ref,
    sine_ref,
    out_ref,
    out_weight,
    first_near_send,
    first_near_recv,
    first_far_send,
    first_far_recv,
    memory_pair,
    mixed,
    second_near_send,
    second_near_recv,
    second_far_send,
    second_far_recv,
    first_total,
    total,
    bias,
    weight_sem,
    near_send_sem,
    near_recv_sem,
    far_send_sem,
    far_recv_sem,
    pair_send_sem,
    pair_recv_sem,
    piece_near_send,
    piece_near_recv,
    piece_far_send,
    piece_far_recv,
    out_send_sem,
    out_recv_sem,
):
    me = lax.axis_index("gx")
    core = lax.axis_index("gy")
    mate = 1 - core
    columns_of = count // 2
    column, row = me // 2, lax.rem(me, 2)
    neighbour = column * 2 + 1 - row
    length, width = query_part.shape[1], query_part.shape[2]
    span = out_ref.shape[2]
    blocks = span // width
    norm = 1.0 / math.sqrt(width)
    chunk = 2 * width
    mesh_ids = pl.DeviceIdType.MESH

    load = pltpu.make_async_copy(out_weight_hbm, out_weight, weight_sem)
    load.start()

    def column_at(step):
        if columns_of == 4:
            return lax.rem(column + 2 + 3 * step + 3 * ((step * (step - 1)) // 2), 4)
        return lax.rem(column + 1 + step, columns_of)

    barrier = pltpu.get_barrier_semaphore()
    pl.semaphore_signal(barrier, inc=1, device_id={"gy": mate}, device_id_type=mesh_ids)
    pl.semaphore_signal(barrier, inc=1, device_id={"gx": neighbour}, device_id_type=mesh_ids)
    for step in range(columns_of - 1):
        pl.semaphore_signal(
            barrier,
            inc=1,
            device_id={"gx": column_at(step) * 2 + row},
            device_id_type=mesh_ids,
        )
    pl.semaphore_wait(barrier, columns_of + 1)

    small_signs = sign_ref[:width, :width]

    def first_near_copy(kind, step):
        return pltpu.make_async_remote_copy(
            src_ref=first_near_send.at[kind, step],
            dst_ref=first_near_recv.at[kind, step],
            send_sem=near_send_sem.at[kind, step],
            recv_sem=near_recv_sem.at[kind, step],
            device_id={"gx": neighbour},
            device_id_type=mesh_ids,
        )

    def first_far_copy(kind, step):
        return pltpu.make_async_remote_copy(
            src_ref=first_far_send.at[kind, step],
            dst_ref=first_far_recv.at[kind, step],
            send_sem=far_send_sem.at[kind, step],
            recv_sem=far_recv_sem.at[kind, step],
            device_id={"gx": column_at(step) * 2 + row},
            device_id_type=mesh_ids,
        )

    def pair_copy(ref, place):
        return pltpu.make_async_remote_copy(
            src_ref=ref.at[core],
            dst_ref=ref.at[core],
            send_sem=pair_send_sem.at[place],
            recv_sem=pair_recv_sem.at[place],
            device_id={"gy": mate},
            device_id_type=mesh_ids,
        )

    def query_term(target):
        scale = power(-query_exponent[0, target], width)
        return saturate(turn(query_part[target], small_signs, norm) * scale)

    def memory_term(target):
        scale = power(-partial_exponent[core, target], width)
        return saturate(turn(memory_part[core, target], small_signs, norm) * scale)

    terms = (memory_term, query_term)

    def first_near(step, carry):
        target = column_at(step) * 2 + 1 - row
        for kind, term in enumerate(terms):
            first_near_send[kind, step] = term(target).astype(jnp.bfloat16)
            first_near_copy(kind, step).start()
        return carry

    def first_joined(kind, step):
        term = terms[kind](column_at(step) * 2 + row)
        first_near_copy(kind, step).wait_recv()
        return term + first_near_recv[kind, step].astype(jnp.float32)

    def first_far(step, carry):
        first_near(step + 1, 0)
        for kind in range(2):
            first_far_send[kind, step] = first_joined(kind, step).astype(jnp.bfloat16)
            first_far_copy(kind, step).start()
        return carry

    first_near(0, 0)
    lax.fori_loop(0, columns_of - 1, first_far, 0)
    for kind in range(2):
        first_total[kind] = first_joined(kind, columns_of - 1)

    rows = lax.broadcasted_iota(jnp.int32, (length, length), 0)
    columns = lax.broadcasted_iota(jnp.int32, (length, length), 1)
    documents = jnp.broadcast_to(document_row[...], (length, length)).astype(jnp.float32)
    allowed = (rows >= columns) & (documents.T == documents)
    bias[...] = jnp.where(allowed, 0.0, -jnp.inf)

    def first_sum(kind, step):
        first_far_copy(kind, step).wait_recv()
        first_total[kind] += first_far_recv[kind, step].astype(jnp.float32)

    for step in range(columns_of - 1):
        first_sum(0, step)
        if step + 2 < columns_of:
            first_sum(1, step)

    level_ratio = power(partial_exponent[core, me] - summed_exponent[core, me], width)
    level = saturate(first_total[0] * level_ratio)
    memory = turn(level * power(summed_exponent[core, me], width), small_signs, norm)
    turned = memory * cosine_ref[...] + pltpu.roll(memory, width // 2, 1) * sine_ref[...]
    memory_pair[core] = jnp.where(core == 0, turned, memory).astype(jnp.bfloat16)
    pair_copy(memory_pair, 0).start()
    first_sum(1, columns_of - 2)
    query = turn(first_total[1] * power(query_exponent[0, me], width), small_signs, norm)
    query = query * cosine_ref[...] + pltpu.roll(query, width // 2, 1) * sine_ref[...]
    query = query.astype(jnp.bfloat16)
    pair_copy(memory_pair, 0).wait_recv()

    scores = lax.dot_general(
        query, memory_pair[0], (((1,), (1,)), ((), ())), preferred_element_type=jnp.float32
    ) * (1.0 / math.sqrt(width))
    scores = scores + bias[...]
    exponentials = jnp.exp(scores - jnp.max(scores, axis=-1, keepdims=True))
    weights = exponentials / jnp.sum(exponentials, axis=-1, keepdims=True)
    mixed[core] = jnp.dot(
        weights.astype(jnp.bfloat16), memory_pair[1], preferred_element_type=jnp.float32
    ).astype(jnp.bfloat16)
    pair_copy(mixed, 1).start()
    load.wait()
    pair_copy(mixed, 1).wait_recv()

    def row_of(exponents):
        return jnp.concatenate([power(exponent, width) for exponent in exponents], axis=1)

    def second_term(target, part):
        start = pl.multiple_of((target * (span // chunk) + part) * chunk, chunk)
        both = jnp.concatenate([mixed[0], mixed[1]], axis=1)
        product = jnp.dot(
            both, out_weight[:, pl.ds(start, chunk)], preferred_element_type=jnp.float32
        )
        block = target * blocks + part * 2
        scale = row_of([-out_exponent[0, block], -out_exponent[0, block + 1]])
        return saturate(turn(product, sign_ref[...], norm) * scale)

    parts = span // chunk
    ahead = parts
    near_total, far_total = columns_of * parts, (columns_of - 1) * parts

    def piece_copy(kind, piece):
        send, recv, send_sem, recv_sem, target = {
            "near": (second_near_send, second_near_recv, piece_near_send, piece_near_recv, None),
            "far": (second_far_send, second_far_recv, piece_far_send, piece_far_recv, 1),
        }[kind]
        if target is None:
            target = neighbour
        else:
            target = column_at(piece // parts) * 2 + row
        return pltpu.make_async_remote_copy(
            src_ref=send.at[piece],
            dst_ref=recv.at[piece],
            send_sem=send_sem.at[piece],
            recv_sem=recv_sem.at[piece],
            device_id={"gx": target},
            device_id_type=mesh_ids,
        )

    def second_near(piece, carry):
        target = column_at(piece // parts) * 2 + 1 - row
        second_near_send[piece] = second_term(target, piece % parts).astype(jnp.bfloat16)
        piece_copy("near", piece).start()
        return carry

    def second_joined(piece):
        term = second_term(column_at(piece // parts) * 2 + row, piece % parts)
        piece_copy("near", piece).wait_recv()
        return term + second_near_recv[piece].astype(jnp.float32)

    def second_far(piece, carry):
        second_near(piece + ahead, 0)
        second_far_send[piece] = second_joined(piece).astype(jnp.bfloat16)
        piece_copy("far", piece).start()
        return carry

    lax.fori_loop(0, ahead, second_near, 0)
    lax.fori_loop(0, far_total, second_far, 0)
    lax.fori_loop(far_total + ahead, near_total, second_near, 0)

    def second_own(part, carry):
        total[part] = second_joined(far_total + part)
        return carry

    lax.fori_loop(0, parts, second_own, 0)

    def second_sum(piece, carry):
        piece_copy("far", piece).wait_recv()
        total[piece % parts] += second_far_recv[piece].astype(jnp.float32)
        return carry

    lax.fori_loop(0, far_total - parts, second_sum, 0)

    def out_copy(part):
        place = slice(part * chunk, (part + 1) * chunk)
        return pltpu.make_async_remote_copy(
            src_ref=out_ref.at[core, :, place],
            dst_ref=out_ref.at[core, :, place],
            send_sem=out_send_sem.at[part],
            recv_sem=out_recv_sem.at[part],
            device_id={"gy": mate},
            device_id_type=mesh_ids,
        )

    for part in range(parts):
        second_sum(far_total - parts + part, 0)
        summed = [out_exponent[0, me * blocks + part * 2 + i] for i in range(2)]
        ending = [relevel[core, part * 2 + i] for i in range(2)]
        ratio = row_of([start - end for start, end in zip(summed, ending)])
        level = saturate(total[part] * ratio) * row_of(ending)
        out_ref[core, :, part * chunk : (part + 1) * chunk] = turn(
            level, sign_ref[...], norm
        ).astype(jnp.bfloat16)
        out_copy(part).start()

    def drain_near(step, carry):
        first_near_copy(0, step).wait_send()
        first_near_copy(1, step).wait_send()
        return carry

    def drain_far(step, carry):
        first_far_copy(0, step).wait_send()
        first_far_copy(1, step).wait_send()
        return carry

    def drain_near_piece(piece, carry):
        piece_copy("near", piece).wait_send()
        return carry

    def drain_far_piece(piece, carry):
        piece_copy("far", piece).wait_send()
        return carry

    lax.fori_loop(0, near_total, drain_near_piece, 0)
    lax.fori_loop(0, far_total, drain_far_piece, 0)
    lax.fori_loop(0, columns_of, drain_near, 0)
    lax.fori_loop(0, columns_of - 1, drain_far, 0)
    pair_copy(memory_pair, 0).wait_send()
    pair_copy(mixed, 1).wait_send()
    for part in range(parts):
        out_copy(part).wait()


def body(
    tokens,
    query_weight,
    key_value_projection_weight,
    output_weight,
    document_ids,
    query_exponent,
    key_value_partial_exponents,
    key_value_summed_exponents,
    output_exponent,
    output_relevel,
):
    count = lax.axis_size("gx")
    length = tokens.shape[0]
    width = query_weight.shape[3]
    heads = query_weight.shape[1]
    memory_heads = key_value_projection_weight.shape[2]
    span = output_weight.shape[1] // count
    even = count % 2 == 0 and lax.axis_size("gy") == 2 and span % (2 * width) == 0
    if not (even and count == heads == memory_heads):
        return plain_body(
            tokens,
            query_weight,
            key_value_projection_weight,
            output_weight,
            document_ids,
            query_exponent,
            key_value_partial_exponents,
            key_value_summed_exponents,
            output_exponent,
            output_relevel,
        )
    query_part = jnp.einsum(
        "sd,dpe->pse", tokens, query_weight[:, :, 0, :], preferred_element_type=jnp.float32
    )
    memory_part = jnp.einsum(
        "sd,dcne->cnse", tokens, key_value_projection_weight, preferred_element_type=jnp.float32
    )
    cosine, sine = rotary_tables(length, width)
    vmem = pl.BlockSpec(memory_space=pltpu.VMEM)
    smem = pl.BlockSpec(memory_space=pltpu.SMEM)
    half = count // 2
    parts = span // (2 * width)
    bf16 = jnp.bfloat16
    halves = pl.pallas_call(
        functools.partial(fused_kernel, count),
        out_shape=jax.ShapeDtypeStruct((2, length, span), bf16),
        in_specs=[vmem, vmem, pl.BlockSpec(memory_space=pl.ANY), vmem] + [smem] * 5 + [vmem] * 3,
        out_specs=vmem,
        scratch_shapes=[
            pltpu.VMEM(output_weight.shape, bf16),
            pltpu.VMEM((2, half, length, width), bf16),
            pltpu.VMEM((2, half, length, width), bf16),
            pltpu.VMEM((2, half - 1, length, width), bf16),
            pltpu.VMEM((2, half - 1, length, width), bf16),
            pltpu.VMEM((2, length, width), bf16),
            pltpu.VMEM((2, length, width), bf16),
            pltpu.VMEM((half * parts, length, 2 * width), bf16),
            pltpu.VMEM((half * parts, length, 2 * width), bf16),
            pltpu.VMEM(((half - 1) * parts, length, 2 * width), bf16),
            pltpu.VMEM(((half - 1) * parts, length, 2 * width), bf16),
            pltpu.VMEM((2, length, width), jnp.float32),
            pltpu.VMEM((parts, length, 2 * width), jnp.float32),
            pltpu.VMEM((length, length), jnp.float32),
            pltpu.SemaphoreType.DMA,
            pltpu.SemaphoreType.DMA((2, half)),
            pltpu.SemaphoreType.DMA((2, half)),
            pltpu.SemaphoreType.DMA((2, half - 1)),
            pltpu.SemaphoreType.DMA((2, half - 1)),
            pltpu.SemaphoreType.DMA((2,)),
            pltpu.SemaphoreType.DMA((2,)),
            pltpu.SemaphoreType.DMA((half * parts,)),
            pltpu.SemaphoreType.DMA((half * parts,)),
            pltpu.SemaphoreType.DMA(((half - 1) * parts,)),
            pltpu.SemaphoreType.DMA(((half - 1) * parts,)),
            pltpu.SemaphoreType.DMA((parts,)),
            pltpu.SemaphoreType.DMA((parts,)),
        ],
        compiler_params=pltpu.CompilerParams(
            collective_id=0, has_side_effects=True, vmem_limit_bytes=40 * 1024 * 1024
        ),
    )(
        query_part,
        memory_part,
        output_weight,
        document_ids[None, :],
        query_exponent.T,
        key_value_partial_exponents,
        key_value_summed_exponents,
        output_exponent,
        output_relevel,
        jnp.asarray(paired_signs(width), bf16),
        jnp.asarray(cosine),
        jnp.asarray(sine),
    )
    return halves.transpose(1, 0, 2)


def solution(mesh):
    return jax.shard_map(
        body,
        mesh=mesh,
        in_specs=(
            P("groups", "gx"),
            P("gx", None, "gy", None),
            P("gx", None, None, None),
            P("gx", "gy"),
            P("groups"),
            P(None, "gy"),
            P(),
            P(),
            P("gy", None),
            P(None, "gx"),
        ),
        out_specs=P("groups", None, "gx"),
        check_vma=False,
    )
```
